256 devices in a mesh: space: 16 (over x, y), spec: 16 (over z, core).
Axes of the slice: x: 4, y: 4, z: 8, core: 2. Of those that a mesh axis runs over, the one named last changes fastest.
Arguments:
- spectrum: float32 [624, 262144], P('spec', 'space'), may hold values from 0.05 to 2
- wind_speed: float32 [262144], P('space'), may hold values from 2 to 25
- wind_dir: float32 [262144], P('space'), may hold values from -3.140625 to 3.140625
- counts: int32 [2048], P('space'), may hold values from 0 to 128, as said below
- send_list: int32 [4096], P('space'), may hold values from 0 to 16383, as said below
- neighbors: int32 [4, 262144], P(None, 'space'), may hold values from 0 to 16639, as said below
- neighbor_mask: int32 [4, 262144], P(None, 'space'), may hold values from 0 to 1
Outputs:
- spectrum_next: float32 [624, 262144], P('spec', 'space')
The draws below stay inside these ranges and needn't reach their ends.
Inputs may be any that keep to these rules, and one draw needn't show every extreme that they name: The sea points of a tile fill its first counts slots and the other slots are empty. The counts of the 128 tiles of one index of space sum to at most 10240, and to exactly 10240 on at least one index. `send_list`: for each index of space, entries 0 to 127 name live slots of its first tile and entries 128 to 255 live slots of its last tile, in an order of their own; entry e of either half is padding (slot 0) where e is not below the count of that tile. `neighbors`: where the mask is 1, a code below 16384 names a live local slot and a larger code names an entry that is not padding; a slot that is not live has all its masks 0. Where the mask is 1, a west or east code names a slot of the slot's own tile, a south code a slot of the tile before it (an entry below 16512 for a device's first tile), and a north code a slot of the tile after it (an entry of 16512 or more for a device's last tile).
All inputs are finite; a program needn't handle non-finite values.
Results may differ from the reference program's by a relative error of at most 0.0003.
Values sent between devices are 32-bit elements; how exact they have to be, the bound alone decides.
No kernel may reach another device: no remote copies, remote signals or barrier semaphores. Data moves between devices by JAX's collectives and lax.ppermute only.
A program may use at most 128 MiB of HBM per device.

```python
import math
from functools import partial
import jax
import jax.numpy as jnp
import numpy as np
from jax import lax

ND = 24
NF = 26
TILE = 128
TILES_DEV = 128
K = 624
PDEV = 16384
P_SIZE = 262144
SEA_DEV = 10240
N_SPACE = 16


def geometry(key):
    key_total, key_full, key_move, key_order = jax.random.split(jax.random.fold_in(key, 31), 4)
    dev_total = jax.random.randint(key_total, (N_SPACE,), SEA_DEV // 2, SEA_DEV + 1)
    full_dev = jax.random.randint(key_full, (), 0, N_SPACE)
    dev_total = jnp.where(jnp.arange(N_SPACE) == full_dev, SEA_DEV, dev_total)
    base_count = dev_total // TILES_DEV
    remainder = dev_total % TILES_DEV
    tile_ids = jnp.arange(TILES_DEV)
    tile_fill = base_count[:, None] + (tile_ids[None, :] < remainder[:, None]).astype(jnp.int32)
    spread = jnp.minimum(base_count - 2, TILE - base_count - 2)
    moved_amount = jax.random.randint(key_move, (N_SPACE, TILES_DEV // 2), 0, spread[:, None] + 1)
    paired = jnp.stack([moved_amount, -moved_amount], axis=2).reshape(N_SPACE, TILES_DEV)
    tile_fill = (tile_fill + paired).astype(jnp.int32)
    slot_ids = jnp.arange(TILE, dtype=jnp.int32)
    slot_pos = slot_ids[None, None, :]
    tile_pos = tile_ids[None, :, None]
    fill_here = tile_fill[:, :, None]
    dead_slot = slot_pos >= fill_here
    scores = jax.random.randint(key_order, (N_SPACE, TILES_DEV, TILE), 0, 1 << 20) * TILE + slot_pos
    scores = scores + dead_slot.astype(jnp.int32) * (1 << 28)
    place_to_slot = jnp.argsort(scores, axis=2).astype(jnp.int32)
    slot_to_place = jnp.argsort(place_to_slot, axis=2).astype(jnp.int32)
    place_ids = slot_pos + jnp.zeros((N_SPACE, 1, 1), jnp.int32)
    first_rows = jnp.where(place_ids[:, 0, :] < tile_fill[:, 0][:, None], place_to_slot[:, 0, :], 0)
    last_rows = jnp.where(place_ids[:, 0, :] < tile_fill[:, TILES_DEV - 1][:, None], place_to_slot[:, TILES_DEV - 1, :] + (TILES_DEV - 1) * TILE, 0)
    send_rows = jnp.stack([first_rows, last_rows], axis=1).astype(jnp.int32).reshape(N_SPACE * 2 * TILE)
    place = slot_to_place
    is_sea = slot_pos < fill_here
    own_slot = tile_pos * TILE + slot_pos
    west_slot = jnp.take_along_axis(place_to_slot, jnp.clip(place - 1, 0, TILE - 1), axis=2)
    east_slot = jnp.take_along_axis(place_to_slot, jnp.clip(place + 1, 0, TILE - 1), axis=2)
    prev_slot = jnp.take_along_axis(jnp.roll(place_to_slot, 1, axis=1), place, axis=2)
    next_slot = jnp.take_along_axis(jnp.roll(place_to_slot, -1, axis=1), place, axis=2)
    west_ok = is_sea & (place >= 1)
    east_ok = is_sea & (place + 1 < fill_here)
    prev_fill = jnp.roll(tile_fill, 1, axis=1)
    next_fill = jnp.roll(tile_fill, -1, axis=1)
    lower_last = jnp.roll(tile_fill[:, TILES_DEV - 1], 1)
    upper_first = jnp.roll(tile_fill[:, 0], -1)
    south_code = jnp.where(tile_pos >= 1, (tile_pos - 1) * TILE + prev_slot, PDEV + place)
    south_fill = jnp.where(tile_pos >= 1, prev_fill[:, :, None], lower_last[:, None, None])
    south_ok = is_sea & (place < south_fill)
    north_code = jnp.where(tile_pos <= TILES_DEV - 2, (tile_pos + 1) * TILE + next_slot, PDEV + TILE + place)
    north_fill = jnp.where(tile_pos <= TILES_DEV - 2, next_fill[:, :, None], upper_first[:, None, None])
    north_ok = is_sea & (place < north_fill)
    masks = jnp.stack([west_ok, east_ok, south_ok, north_ok], axis=0)
    codes = jnp.stack([jnp.where(west_ok, tile_pos * TILE + west_slot, own_slot), jnp.where(east_ok, tile_pos * TILE + east_slot, own_slot), jnp.where(south_ok, south_code, own_slot), jnp.where(north_ok, north_code, own_slot)], axis=0)
    codes = codes.astype(jnp.int32).reshape(4, N_SPACE * PDEV)
    masks = masks.astype(jnp.int32).reshape(4, N_SPACE * PDEV)
    return (tile_fill.reshape(N_SPACE * TILES_DEV), send_rows, codes, masks)


def draw_counts(key, part):
    return geometry(key)[0]


def draw_send_list(key, part):
    return geometry(key)[1]


def draw_neighbors(key, part):
    return geometry(key)[2]


def draw_neighbor_mask(key, part):
    return geometry(key)[3]


def block_levels(rng, shape, shards, least, top_value):
    loudness, own = 1.0, jax.random.fold_in(rng, 6)
    for axis_at, parts in shards:
        heights = jnp.exp(jax.random.uniform(jax.random.fold_in(own, axis_at), (parts,), jnp.float32, least / len(shards), top_value / len(shards)))
        loudness = loudness * jnp.repeat(heights, shape[axis_at] // parts).reshape([-1 if axis == axis_at else 1 for axis in range(len(shape))])
    return loudness


def setup_inputs(seed: int = 0) -> dict:
    splits = jax.random.split(jax.random.key(seed), 8)
    spectrum = jnp.clip(jnp.exp(math.log(2.0) - 3.6888794 * jax.random.uniform(splits[0], (K, P_SIZE), jnp.float32) ** block_levels(splits[0], (K, P_SIZE), ((0, 16), (1, 16)), -0.2, 0.2)), 0.05, 2.0)
    wind_speed = jnp.clip(2.0 + 23.0 * jax.random.uniform(splits[1], (P_SIZE,), jnp.float32) ** block_levels(splits[1], (P_SIZE,), ((0, 16),), -0.2, 0.2), 2.0, 25.0)
    wind_dir = jnp.clip(jax.random.uniform(splits[2], (P_SIZE,), jnp.float32, -3.140625, 3.140625), -3.140625, 3.140625)
    counts = draw_counts(jax.random.fold_in(splits[7], 71), 0)
    send_list = draw_send_list(jax.random.fold_in(splits[7], 71), 0)
    neighbors = draw_neighbors(jax.random.fold_in(splits[7], 71), 0)
    neighbor_mask = draw_neighbor_mask(jax.random.fold_in(splits[7], 71), 0)
    return {"spectrum": spectrum, "wind_speed": wind_speed, "wind_dir": wind_dir, "counts": counts, "send_list": send_list, "neighbors": neighbors, "neighbor_mask": neighbor_mask}


LOG_RATIO = math.log(1.1)
FREQ_LOW = 0.05
EPS = 1e-6
PLUS_FACTOR = 1.0 / 1.25 ** 4
MINUS_FACTOR = 1.0 / 0.75 ** 4
CROSS_FACTOR = 1.0 / 0.9375 ** 4


def component_tables(comp_index):
    band_level = (comp_index // ND).astype(jnp.float32)
    heading = ((comp_index % ND).astype(jnp.float32) + 0.5) * (2.0 * math.pi / ND)
    frequency = FREQ_LOW * jnp.exp(LOG_RATIO * band_level)
    courant = 0.6 * jnp.exp(-LOG_RATIO * band_level)
    return frequency, heading, courant


def interaction_table(dir_count, freq_count):
    comp_total = dir_count * freq_count
    matrix = np.zeros((2 * comp_total, comp_total), np.float32)
    shifts = ((math.log(1.25) / math.log(1.1), 33.56 * dir_count / 360.0),
              (math.log(0.75) / math.log(1.1), 11.48 * dir_count / 360.0))
    for which_half, (band_shift, turning) in enumerate(shifts):
        for band_level in range(freq_count):
            band_place = band_level + band_shift
            low_band = math.floor(band_place)
            frac_band = band_place - low_band
            for mirror in (1.0, -1.0):
                for heading in range(dir_count):
                    dir_place = heading + mirror * turning
                    low_dir = math.floor(dir_place)
                    frac_dir = dir_place - low_dir
                    row_index = which_half * comp_total + band_level * dir_count + heading
                    for band_step, band_weight in ((0, 1.0 - frac_band), (1, frac_band)):
                        source_band = low_band + band_step
                        if 0 <= source_band < freq_count:
                            for dir_step, dir_weight in ((0, 1.0 - frac_dir), (1, frac_dir)):
                                source_dir = (low_dir + dir_step) % dir_count
                                matrix[row_index, source_band * dir_count + source_dir] += 0.5 * band_weight * dir_weight
    return matrix


def sources(pair_table, frequency, spectra):
    freq_col = frequency[:, None]
    mean_freq = jnp.mean(frequency)
    energy_sum = jnp.mean(spectra, axis=0) + EPS
    first_moment = (jnp.mean(freq_col * spectra, axis=0) + EPS * mean_freq) / energy_sum
    steepness = energy_sum * (first_moment / mean_freq) ** 4
    decay = 0.3 * (freq_col / first_moment) * steepness ** 2
    shifted = jnp.dot(pair_table, spectra, precision=lax.Precision.HIGHEST)
    upper_part = shifted[:K]
    lower_part = shifted[K:]
    exchange_term = 0.05 * (freq_col / first_moment) * (
        spectra * spectra * (upper_part * PLUS_FACTOR + lower_part * MINUS_FACTOR)
        - 2.0 * CROSS_FACTOR * spectra * upper_part * lower_part)
    return spectra * jnp.exp(-decay) + exchange_term


def reference(spectrum, wind_speed, wind_dir, counts, send_list, neighbors, neighbor_mask):
    slot_total = N_SPACE * PDEV
    position = jnp.arange(TILE, dtype=jnp.int32)
    wet_slot = (position[None, :] < counts[:, None]).reshape(slot_total).astype(jnp.float32)
    energy = spectrum * wet_slot[None, :]
    owner_dev = jnp.arange(slot_total, dtype=jnp.int32) // PDEV
    lower_dev = (owner_dev + N_SPACE - 1) % N_SPACE
    upper_dev = (owner_dev + 1) % N_SPACE
    list_rows = send_list.reshape(N_SPACE, 2 * TILE)
    from_below = jnp.clip(neighbors - PDEV, 0, TILE - 1) + TILE
    from_above = jnp.clip(neighbors - PDEV - TILE, 0, TILE - 1)
    slot_below = lower_dev[None, :] * PDEV + list_rows[lower_dev[None, :], from_below]
    slot_above = upper_dev[None, :] * PDEV + list_rows[upper_dev[None, :], from_above]
    target = jnp.where(neighbors < PDEV, owner_dev[None, :] * PDEV + neighbors,
                       jnp.where(neighbors < PDEV + TILE, slot_below, slot_above)).astype(jnp.int32)
    frequency, heading, courant = component_tables(jnp.arange(K, dtype=jnp.int32))
    east_speed = (courant * jnp.cos(heading))[:, None]
    north_speed = (courant * jnp.sin(heading))[:, None]
    weights = (jnp.maximum(east_speed, 0.0), jnp.maximum(-east_speed, 0.0),
               jnp.maximum(north_speed, 0.0), jnp.maximum(-north_speed, 0.0))
    advected = energy
    for direction in range(4):
        nearby = jnp.take(energy, target[direction], axis=1) * neighbor_mask[direction].astype(jnp.float32)[None, :]
        advected = advected - weights[direction] * (energy - nearby)
    advected = advected * wet_slot[None, :]
    wind_drive = wind_speed[None, :] * frequency[:, None] * jnp.cos(heading[:, None] - wind_dir[None, :]) / 1.56 - 1.0
    growth = advected * jnp.exp(0.08 * jnp.maximum(wind_drive, 0.0))
    pair_table = jnp.asarray(interaction_table(ND, NF), dtype=jnp.float32)
    blocks = growth.reshape(K, N_SPACE, PDEV).transpose(1, 0, 2)
    updated = lax.map(partial(sources, pair_table, frequency), blocks)
    updated = updated.transpose(1, 0, 2).reshape(K, slot_total)
    return updated * wet_slot[None, :]
```

```python
import math
from functools import partial

import jax
import jax.numpy as jnp
import ml_dtypes
import numpy as np
from jax import lax
from jax.experimental import pallas as pl
from jax.experimental.pallas import tpu as pltpu
from jax.sharding import PartitionSpec as P

ND = 24
NF = 26
TILE = 128
K = 624
NT = 128
ROWS = 39
PAD = 40
CHIPS = 8
CHIP_ROWS = 78
N_SPACE = 16
N_SPEC = 16

LOG_RATIO = math.log(1.1)
FREQ_LOW = 0.05
EPS = 1e-06
PLUS_FACTOR = 1.0 / 1.25**4
MINUS_FACTOR = 1.0 / 0.75**4
CROSS_FACTOR = 1.0 / 0.9375**4

CHUNKS = (40, 40)
FIRST = CHUNKS[0] * TILE
SEA_TILES = sum(CHUNKS)

RELAY = 24
FAR = 8
PIECES = 6 * PAD + RELAY + FAR


def tables():
    k = np.arange(K)
    level = (k // ND).astype(np.float64)
    heading = ((k % ND) + 0.5) * (2.0 * math.pi / ND)
    frequency = FREQ_LOW * np.exp(LOG_RATIO * level)
    courant = 0.6 * np.exp(-LOG_RATIO * level)
    return frequency, heading, courant


FREQ = tables()[0]
MEAN_FREQ = float(FREQ.mean())


def component_params():
    frequency, heading, courant = tables()
    east = courant * np.cos(heading)
    north = courant * np.sin(heading)
    cols = (
        0.08 * frequency * np.cos(heading) / 1.56,
        0.08 * frequency * np.sin(heading) / 1.56,
        np.abs(east),
        np.abs(north),
        1.0 - np.abs(east) - np.abs(north),
        (east > 0).astype(np.float64),
        (north > 0).astype(np.float64),
        frequency,
    )
    out = np.zeros((N_SPEC, PAD, TILE), np.float32)
    for lane, col in enumerate(cols):
        out[:, :ROWS, lane] = col.reshape(N_SPEC, ROWS)
    return out


def interaction_table(dir_count, freq_count):
    comp_total = dir_count * freq_count
    matrix = np.zeros((2 * comp_total, comp_total), np.float32)
    shifts = (
        (math.log(1.25) / math.log(1.1), 33.56 * dir_count / 360.0),
        (math.log(0.75) / math.log(1.1), 11.48 * dir_count / 360.0),
    )
    for which_half, (band_shift, turning) in enumerate(shifts):
        for band_level in range(freq_count):
            band_place = band_level + band_shift
            low_band = math.floor(band_place)
            frac_band = band_place - low_band
            for mirror in (1.0, -1.0):
                for heading in range(dir_count):
                    dir_place = heading + mirror * turning
                    low_dir = math.floor(dir_place)
                    frac_dir = dir_place - low_dir
                    row_index = which_half * comp_total + band_level * dir_count + heading
                    for band_step, band_weight in ((0, 1.0 - frac_band), (1, frac_band)):
                        source_band = low_band + band_step
                        if 0 <= source_band < freq_count:
                            for dir_step, dir_weight in ((0, 1.0 - frac_dir), (1, frac_dir)):
                                source_dir = (low_dir + dir_step) % dir_count
                                matrix[row_index, source_band * dir_count + source_dir] += (
                                    0.5 * band_weight * dir_weight
                                )
    return matrix


def piece_columns(dev):
    chip, core = divmod(dev, 2)

    def rows(offset, which):
        first = ((chip + offset) % CHIPS) * CHIP_ROWS + ROWS * which
        return list(range(first, first + ROWS)) + [-1]

    cols = []
    for offset in (0, -1, 1):
        cols += rows(offset, core) + rows(offset, 1 - core)
    below = rows(-2, 1)
    turn = 6 * (chip % 4)
    cols += [below[21 - turn] if turn else -1, -1, -1, -1] + below[20:40]
    above = rows(2, 0)
    cols += [-1] + above[9:12] + above[3:6] + [-1]
    return cols


def interaction_weights():
    table = interaction_table(ND, NF)
    out = np.zeros((N_SPEC, 4 * PAD, PIECES), np.float32)
    for dev in range(N_SPEC):
        cols = np.array(piece_columns(dev))
        held = cols[cols >= 0]
        assert len(cols) == PIECES and len(set(held.tolist())) == len(held)
        for half, factor in ((0, PLUS_FACTOR), (1, MINUS_FACTOR)):
            for slot, owner in enumerate((dev, dev ^ 1)):
                want = table[half * K + ROWS * owner : half * K + ROWS * owner + ROWS]
                got = np.where(cols >= 0, want[:, np.maximum(cols, 0)], 0.0)
                assert np.array_equal((got != 0).sum(1), (want != 0).sum(1))
                at = half * 2 * PAD + slot * PAD
                out[dev, at : at + ROWS] = got * factor
    high = out.astype(ml_dtypes.bfloat16)
    low = (out - high.astype(np.float32)).astype(ml_dtypes.bfloat16)
    return np.concatenate([high, low], axis=1)


VMEM = pl.BlockSpec(memory_space=pltpu.VMEM)
SMEM = pl.BlockSpec(memory_space=pltpu.SMEM)
PARAMS = pltpu.CompilerParams(vmem_limit_bytes=48 * 1024 * 1024)


def lanes(tile):
    return pl.ds(pl.multiple_of(tile * TILE, TILE), TILE)


def gather(x, index):
    return jnp.take_along_axis(x, index, axis=1, mode="promise_in_bounds")


def edges_kernel(first_ref, last_ref, list_ref, low_ref, high_ref):
    for src, row, out in ((first_ref, 0, low_ref), (last_ref, 1, high_ref)):
        index = jnp.broadcast_to(list_ref[row : row + 1, :] & (TILE - 1), (PAD, TILE))
        out[...] = gather(src[...], index)


def edges(spectrum, send_list):
    return pl.pallas_call(
        edges_kernel,
        grid=(1,),
        in_specs=[
            pl.BlockSpec((PAD, TILE), lambda i: (0, 0)),
            pl.BlockSpec((PAD, TILE), lambda i: (0, NT - 1)),
            pl.BlockSpec((2, TILE), lambda i: (0, 0)),
        ],
        out_specs=[pl.BlockSpec((PAD, TILE), lambda i: (0, 0))] * 2,
        out_shape=[jax.ShapeDtypeStruct((PAD, TILE), jnp.float32)] * 2,
        name="edges",
    )(spectrum, spectrum, send_list.reshape(2, TILE))


def advect_kernel(first, last, base, tiles, *refs):
    if last:
        (dev_ref, counts_ref, state_ref, x_ref, code_ref, mask_ref, wa_ref, wb_ref, tab_ref, lower_ref, upper_ref,
         keep_ref, send_ref, par, dst) = refs
    else:
        (dev_ref, counts_ref, x_ref, code_ref, mask_ref, wa_ref, wb_ref, tab_ref,
         keep_ref, send_ref, next_ref, par, dst) = refs
    table = tab_ref[0]
    for i in range(7):
        par[i] = jnp.broadcast_to(table[:, i : i + 1], (PAD, TILE))
    real = lax.broadcasted_iota(jnp.int32, (PAD, TILE), 0) < ROWS
    lane = lax.broadcasted_iota(jnp.int32, (PAD, TILE), 1)

    def process(t, off, before, after):
        own = x_ref[:, lanes(t)]
        code = code_ref[:, lanes(t)] & (TILE - 1)
        sea = mask_ref[:, lanes(t)].astype(jnp.float32)
        to_east = par[5] > 0.5
        to_north = par[6] > 0.5
        near_x = gather(own, jnp.where(to_east, code[0:1], code[1:2]))
        near_x = near_x * jnp.where(to_east, sea[0:1], sea[1:2])
        near_y = gather(jnp.where(to_north, before, after), jnp.where(to_north, code[2:3], code[3:4]))
        near_y = near_y * jnp.where(to_north, sea[2:3], sea[3:4])
        value = own * par[4] + par[2] * near_x + par[3] * near_y
        drive = par[0] * wa_ref[pl.ds(t, 1), :] + par[1] * wb_ref[pl.ds(t, 1), :]
        value = value * jnp.exp(jnp.maximum(drive - 0.08, 0.0))
        value = jnp.where(real, value, 0.0)
        shift = off & (TILE - 1)
        at = (off >> 7) - base + 1
        value = pltpu.roll(value, shift, 1)
        dst[at] = jnp.where(lane < shift, dst[at], value)
        dst[at + 1] = value

    def inner(t, off):
        process(t, off, x_ref[:, lanes(t - 1)], x_ref[:, lanes(t + 1)])
        return off + counts_ref[t]

    limit = (base + tiles) * TILE
    if first:
        t0, off0 = jnp.int32(1), jnp.int32(0)
    else:
        t0, off0 = state_ref[0], state_ref[1]
    if last:
        _, off = lax.while_loop(
            lambda c: c[0] < NT - 1, lambda c: (c[0] + 1, inner(c[0], c[1])), (t0, off0)
        )
        off = jnp.maximum(off, FIRST)
        process(0, off, lower_ref[...], x_ref[:, lanes(1)])
        off = off + counts_ref[0]
        process(NT - 1, off, x_ref[:, lanes(NT - 2)], upper_ref[...])
    else:
        t, off, back = lax.while_loop(
            lambda c: (c[0] < NT - 1) & (c[1] < limit),
            lambda c: (c[0] + 1, inner(c[0], c[1]), c[1]),
            (t0, off0, off0),
        )
        straddles = off > limit
        next_ref[0] = jnp.where(straddles, t - 1, t)
        next_ref[1] = jnp.where(straddles, back, jnp.maximum(off, limit))
    half = tiles // 2
    core = dev_ref[0] & 1

    def emit(j, _):
        keep_ref[:, lanes(j)] = dst[1 + core * half + j]
        send_ref[:, lanes(j)] = dst[1 + (1 - core) * half + j]
        return 0

    lax.fori_loop(0, half, emit, 0)


def advect(first, last, base, tiles, dev, counts, state, spectrum, codes, mask, wa, wb, tab, lower, upper):
    half = tiles // 2 * TILE
    whole = lambda shape: pl.BlockSpec(shape, lambda i, d: (0,) * len(shape))
    tab_spec = pl.BlockSpec((1, PAD, TILE), lambda i, d: (d[0], 0, 0))
    args = [counts] + ([] if first else [state]) + [spectrum, codes, mask, wa, wb, tab]
    specs = [SMEM] + ([] if first else [SMEM])
    specs += [whole((PAD, NT * TILE)), whole((4, NT * TILE)), whole((4, NT * TILE)), whole((NT, TILE)), whole((NT, TILE)), tab_spec]
    outs = [jax.ShapeDtypeStruct((PAD, half), jnp.float32)] * 2
    out_specs = [whole((PAD, half))] * 2
    if last:
        args += [lower, upper]
        specs += [whole((PAD, TILE))] * 2
    else:
        outs = outs + [jax.ShapeDtypeStruct((2,), jnp.int32)]
        out_specs = out_specs + [SMEM]
    return pl.pallas_call(
        partial(advect_kernel, first, last, base, tiles),
        grid_spec=pltpu.PrefetchScalarGridSpec(
            num_scalar_prefetch=1,
            grid=(1,),
            in_specs=specs,
            out_specs=out_specs,
            scratch_shapes=[
                pltpu.VMEM((7, PAD, TILE), jnp.float32),
                pltpu.VMEM((tiles + 4, PAD, TILE), jnp.float32),
            ],
        ),
        out_shape=outs,
        compiler_params=PARAMS,
        name="advect",
    )(dev, *args)


def moments_kernel(dev_ref, mine_ref, other_ref, tab_a, tab_b, out_ref):
    mine, other = mine_ref[...], other_ref[...]
    fa, fb = tab_a[0][:, 7:8], tab_b[0][:, 7:8]
    out_ref[0:1, :] = jnp.sum(mine, axis=0, keepdims=True) + jnp.sum(other, axis=0, keepdims=True)
    out_ref[1:2, :] = jnp.sum(fa * mine, axis=0, keepdims=True) + jnp.sum(fb * other, axis=0, keepdims=True)


def tab_specs():
    return [
        pl.BlockSpec((1, PAD, TILE), lambda i, d: (d[0], 0, 0)),
        pl.BlockSpec((1, PAD, TILE), lambda i, d: (d[0] ^ 1, 0, 0)),
    ]


def moments(dev, mine, other, tab):
    n = mine.shape[1]
    return pl.pallas_call(
        moments_kernel,
        grid_spec=pltpu.PrefetchScalarGridSpec(
            num_scalar_prefetch=1,
            grid=(1,),
            in_specs=[pl.BlockSpec((PAD, n), lambda i, d: (0, 0))] * 2 + tab_specs(),
            out_specs=pl.BlockSpec((2, n), lambda i, d: (0, 0)),
        ),
        out_shape=jax.ShapeDtypeStruct((2, n), jnp.float32),
        compiler_params=PARAMS,
        name="moments",
    )(dev, mine, other, tab, tab)


def far_kernel(dev_ref, mine_ref, other_ref, sum_ref, got_ref, out_ref):
    core = dev_ref[0] & 1
    low = jnp.where(core == 0, mine_ref[...], other_ref[...])
    total = sum_ref[...] + got_ref[...]
    out_ref[0:1, :] = total[0:1]
    out_ref[1:4, :] = low[9:12]
    out_ref[4:7, :] = low[3:6]
    out_ref[7:8, :] = total[1:2]


def far_pack(dev, mine, other, sums, got):
    n = mine.shape[1]
    return pl.pallas_call(
        far_kernel,
        grid_spec=pltpu.PrefetchScalarGridSpec(
            num_scalar_prefetch=1,
            grid=(1,),
            in_specs=[pl.BlockSpec((16, n), lambda i, d: (0, 0))] * 2 + [pl.BlockSpec((2, n), lambda i, d: (0, 0))] * 2,
            out_specs=pl.BlockSpec((FAR, n), lambda i, d: (0, 0)),
        ),
        out_shape=jax.ShapeDtypeStruct((FAR, n), jnp.float32),
        compiler_params=PARAMS,
        name="far_pack",
    )(dev, mine, other, sums, got)


def relay_kernel(dev_ref, mine_ref, other_ref, sent_ref, got_ref, out_ref):
    core = dev_ref[0] & 1
    turn = ((dev_ref[0] >> 1) + 1) & 3
    rows = jnp.where(core == 1, mine_ref[...], other_ref[...])
    out_ref[...] = rows[16:40]
    out_ref[0:1, :] = jnp.where(turn == 1, rows[15:16], jnp.where(turn == 2, rows[9:10], rows[3:4]))
    out_ref[1:2, :] = sent_ref[0:1] + got_ref[0:1]
    out_ref[2:3, :] = sent_ref[7:8] + got_ref[7:8]


def relay_pack(dev, mine, other, sent, got):
    n = mine.shape[1]
    return pl.pallas_call(
        relay_kernel,
        grid_spec=pltpu.PrefetchScalarGridSpec(
            num_scalar_prefetch=1,
            grid=(1,),
            in_specs=[pl.BlockSpec((PAD, n), lambda i, d: (0, 0))] * 2 + [pl.BlockSpec((FAR, n), lambda i, d: (0, 0))] * 2,
            out_specs=pl.BlockSpec((RELAY, n), lambda i, d: (0, 0)),
        ),
        out_shape=jax.ShapeDtypeStruct((RELAY, n), jnp.float32),
        compiler_params=PARAMS,
        name="relay_pack",
    )(dev, mine, other, sent, got)


def sources_kernel(dev_ref, w_ref, tab_a, tab_b, sent_ref, *refs):
    pieces, (mine_out, other_out) = refs[:8], refs[8:]
    relay = pieces[6]
    stacked = jnp.concatenate([p[...] for p in pieces], axis=0)
    high = stacked.astype(jnp.bfloat16)
    low = (stacked - high.astype(jnp.float32)).astype(jnp.bfloat16)
    main = jnp.dot(w_ref[0], high, preferred_element_type=jnp.float32)
    rest = jnp.dot(w_ref[0, : 4 * PAD, :], low, preferred_element_type=jnp.float32)
    shifted = main[: 4 * PAD] + main[4 * PAD :] + rest
    energy_sum = (sent_ref[1:2, :] + relay[1:2, :]) * (1.0 / K) + EPS
    first_moment = ((sent_ref[2:3, :] + relay[2:3, :]) * (1.0 / K) + EPS * MEAN_FREQ) / energy_sum
    ratio = first_moment * (1.0 / MEAN_FREQ)
    ratio = ratio * ratio
    steepness = energy_sum * (ratio * ratio)
    inverse = 1.0 / first_moment
    fade = -0.3 * inverse * (steepness * steepness)
    gain = 0.05 * inverse
    cross = 2.0 * CROSS_FACTOR / (PLUS_FACTOR * MINUS_FACTOR)
    for at, tab, g_ref, out in ((0, tab_a, pieces[0], mine_out), (PAD, tab_b, pieces[1], other_out)):
        freq = tab[0][:, 7:8]
        g = g_ref[...]
        upper = shifted[at : at + PAD]
        lower = shifted[2 * PAD + at : 2 * PAD + at + PAD]
        out[...] = g * (jnp.exp(freq * fade) + (freq * gain) * (g * (upper + lower) - cross * (upper * lower)))


def sources(dev, weights, tab, sent, pieces, block):
    n = sent.shape[1]
    spec = lambda rows: pl.BlockSpec((rows, block), lambda i, d: (0, i))
    return pl.pallas_call(
        sources_kernel,
        grid_spec=pltpu.PrefetchScalarGridSpec(
            num_scalar_prefetch=1,
            grid=(n // block,),
            in_specs=[pl.BlockSpec((1, 8 * PAD, PIECES), lambda i, d: (d[0], 0, 0))]
            + tab_specs()
            + [spec(8)]
            + [spec(PAD)] * 6
            + [spec(RELAY), spec(FAR)],
            out_specs=[spec(PAD)] * 2,
        ),
        out_shape=[jax.ShapeDtypeStruct((PAD, n), jnp.float32)] * 2,
        compiler_params=PARAMS,
        name="sources",
    )(dev, weights, tab, tab, sent, *pieces)


def expand_kernel(dev_ref, counts_ref, *refs):
    count = 2 * len(CHUNKS)
    pieces, out_ref, held = refs[:count], refs[count], refs[count + 1]
    core = dev_ref[0] & 1
    base = 0
    for i, tiles in enumerate(CHUNKS):
        half = tiles // 2
        mine, other = pieces[2 * i], pieces[2 * i + 1]

        def fill(j, _, mine=mine, other=other, base=base, half=half):
            held[base + core * half + j] = mine[:, lanes(j)]
            held[base + (1 - core) * half + j] = other[:, lanes(j)]
            return 0

        lax.fori_loop(0, half, fill, 0)
        base += tiles
    lane = lax.broadcasted_iota(jnp.int32, (PAD, TILE), 1)

    def place(t, off):
        shift = off & (TILE - 1)
        at = off >> 7
        value = jnp.where(lane >= shift, held[at], held[at + 1])
        value = pltpu.roll(value, (TILE - shift) & (TILE - 1), 1)
        value = jnp.where(lane < counts_ref[t], value, 0.0)
        out_ref[:, lanes(t)] = value
        return off + counts_ref[t]

    off = lax.fori_loop(1, NT - 1, place, jnp.int32(0))
    off = jnp.maximum(off, FIRST)
    off = place(0, off)
    place(NT - 1, off)


def expand(dev, counts, pieces):
    whole = lambda shape: pl.BlockSpec(shape, lambda i, d: (0,) * len(shape))
    return pl.pallas_call(
        expand_kernel,
        grid_spec=pltpu.PrefetchScalarGridSpec(
            num_scalar_prefetch=1,
            grid=(1,),
            in_specs=[SMEM] + [whole(p.shape) for p in pieces],
            out_specs=whole((PAD, NT * TILE)),
            scratch_shapes=[pltpu.VMEM((SEA_TILES + 4, PAD, TILE), jnp.float32)],
        ),
        out_shape=jax.ShapeDtypeStruct((ROWS, NT * TILE), jnp.float32),
        compiler_params=PARAMS,
        name="expand",
    )(dev, counts, *pieces)


def per_device(spectrum, wind_speed, wind_dir, counts, send_list, neighbors, neighbor_mask):
    dev = lax.axis_index("spec").astype(jnp.int32).reshape(1)
    tab = jnp.asarray(component_params())
    weights = jnp.asarray(interaction_weights())

    def shift(x, hops):
        return lax.ppermute(x, "spec", [(s, (s + hops) % N_SPEC) for s in range(N_SPEC)])

    def swap(x):
        return lax.ppermute(x, "spec", [(s, s ^ 1) for s in range(N_SPEC)])

    to_lower, to_upper = edges(spectrum, send_list)
    lower = lax.ppermute(to_upper, "space", [(s, (s + 1) % N_SPACE) for s in range(N_SPACE)])
    upper = lax.ppermute(to_lower, "space", [(s, (s - 1) % N_SPACE) for s in range(N_SPACE)])
    wa = (wind_speed * jnp.cos(wind_dir)).reshape(NT, TILE)
    wb = (wind_speed * jnp.sin(wind_dir)).reshape(NT, TILE)

    results = []
    state = None
    base = 0
    for i, tiles in enumerate(CHUNKS):
        last = i == len(CHUNKS) - 1
        got = advect(i == 0, last, base, tiles, dev, counts, state, spectrum, neighbors, neighbor_mask, wa, wb, tab, lower, upper)
        base += tiles
        if last:
            mine, send = got
        else:
            mine, send, state = got
        other = swap(send)
        sums = moments(dev, mine, other, tab)
        far_sums = shift(sums, 8)
        up_mine, down_mine = shift(mine, 2), shift(mine, -2)
        up_other, down_other = shift(other, 2), shift(other, -2)
        sent_far = far_pack(dev, mine, other, sums, far_sums)
        far = shift(sent_far, -4)
        sent = relay_pack(dev, up_mine, up_other, sent_far, far)
        relay = shift(sent, 2)
        mine, other = sources(
            dev, weights, tab, sent, [mine, other, up_mine, up_other, down_mine, down_other, relay, far], 512
        )
        results += [mine, swap(other)]
    return expand(dev, counts, results)


def solution(mesh):
    in_specs = (
        P("spec", "space"),
        P("space"),
        P("space"),
        P("space"),
        P("space"),
        P(None, "space"),
        P(None, "space"),
    )
    out_specs = P("spec", "space")
    return jax.shard_map(
        per_device, mesh=mesh, in_specs=in_specs, out_specs=out_specs, check_vma=False
    )
```

```python
import math
from functools import partial

import jax
import jax.numpy as jnp
import ml_dtypes
import numpy as np
from jax import lax
from jax.experimental import pallas as pl
from jax.experimental.pallas import tpu as pltpu
from jax.sharding import PartitionSpec as P

ND = 24
NF = 26
TILE = 128
K = 624
NT = 128
ROWS = 39
PAD = 40
CHIPS = 8
CHIP_ROWS = 78
N_SPACE = 16
N_SPEC = 16

LOG_RATIO = math.log(1.1)
FREQ_LOW = 0.05
EPS = 1e-06
PLUS_FACTOR = 1.0 / 1.25**4
MINUS_FACTOR = 1.0 / 0.75**4
CROSS_FACTOR = 1.0 / 0.9375**4

CHUNKS = (40, 40)
FIRST = CHUNKS[0] * TILE
SEA_TILES = sum(CHUNKS)
BLOCK = 1280

RELAY = 24
FAR = 4
PIECES = 6 * PAD + RELAY + 8


def tables():
    k = np.arange(K)
    level = (k // ND).astype(np.float64)
    heading = ((k % ND) + 0.5) * (2.0 * math.pi / ND)
    frequency = FREQ_LOW * np.exp(LOG_RATIO * level)
    courant = 0.6 * np.exp(-LOG_RATIO * level)
    return frequency, heading, courant


FREQ = tables()[0]
MEAN_FREQ = float(FREQ.mean())


def component_params():
    frequency, heading, courant = tables()
    east = courant * np.cos(heading)
    north = courant * np.sin(heading)
    cols = (
        0.08 * frequency * np.cos(heading) / 1.56,
        0.08 * frequency * np.sin(heading) / 1.56,
        np.abs(east),
        np.abs(north),
        1.0 - np.abs(east) - np.abs(north),
        (east > 0).astype(np.float64),
        (north > 0).astype(np.float64),
        frequency,
    )
    out = np.zeros((N_SPEC, PAD, TILE), np.float32)
    for lane, col in enumerate(cols):
        out[:, :ROWS, lane] = col.reshape(N_SPEC, ROWS)
    out[:, :, 8] = np.roll(out[:, :, 7], 2, axis=0)
    out[:, :, 9] = np.roll(out[:, :, 7], -2, axis=0)
    return out


def interaction_table(dir_count, freq_count):
    comp_total = dir_count * freq_count
    matrix = np.zeros((2 * comp_total, comp_total), np.float32)
    shifts = (
        (math.log(1.25) / math.log(1.1), 33.56 * dir_count / 360.0),
        (math.log(0.75) / math.log(1.1), 11.48 * dir_count / 360.0),
    )
    for which_half, (band_shift, turning) in enumerate(shifts):
        for band_level in range(freq_count):
            band_place = band_level + band_shift
            low_band = math.floor(band_place)
            frac_band = band_place - low_band
            for mirror in (1.0, -1.0):
                for heading in range(dir_count):
                    dir_place = heading + mirror * turning
                    low_dir = math.floor(dir_place)
                    frac_dir = dir_place - low_dir
                    row_index = which_half * comp_total + band_level * dir_count + heading
                    for band_step, band_weight in ((0, 1.0 - frac_band), (1, frac_band)):
                        source_band = low_band + band_step
                        if 0 <= source_band < freq_count:
                            for dir_step, dir_weight in ((0, 1.0 - frac_dir), (1, frac_dir)):
                                source_dir = (low_dir + dir_step) % dir_count
                                matrix[row_index, source_band * dir_count + source_dir] += (
                                    0.5 * band_weight * dir_weight
                                )
    return matrix


def piece_columns(dev):
    chip, core = divmod(dev, 2)

    def rows(offset, which):
        first = ((chip + offset) % CHIPS) * CHIP_ROWS + ROWS * which
        return list(range(first, first + ROWS)) + [-1]

    cols = []
    for offset in (0, -1, 1):
        cols += rows(offset, core) + rows(offset, 1 - core)
    below = rows(-2, 1)
    turn = 6 * (chip % 4)
    cols += [below[21 - turn] if turn else -1, -1, -1, -1] + below[20:40]
    above = rows(2, 0)
    turn = 6 * ((chip + 1) % 4)
    cols += (above[9:12] if turn == 6 else above[3:6] if turn == 12 else [-1] * 3) + [-1] * 5
    return cols


def interaction_weights():
    table = interaction_table(ND, NF)
    out = np.zeros((N_SPEC, 4 * PAD, PIECES), np.float32)
    for dev in range(N_SPEC):
        cols = np.array(piece_columns(dev))
        held = cols[cols >= 0]
        assert len(cols) == PIECES and len(set(held.tolist())) == len(held)
        for half, factor in ((0, PLUS_FACTOR), (1, MINUS_FACTOR)):
            for slot, owner in enumerate((dev, dev ^ 1)):
                want = table[half * K + ROWS * owner : half * K + ROWS * owner + ROWS]
                got = np.where(cols >= 0, want[:, np.maximum(cols, 0)], 0.0)
                assert np.array_equal((got != 0).sum(1), (want != 0).sum(1))
                at = half * 2 * PAD + slot * PAD
                out[dev, at : at + ROWS] = got * factor
    high = out.astype(ml_dtypes.bfloat16)
    low = (out - high.astype(np.float32)).astype(ml_dtypes.bfloat16)
    return np.concatenate([high, low, high], axis=2)


VMEM = pl.BlockSpec(memory_space=pltpu.VMEM)
SMEM = pl.BlockSpec(memory_space=pltpu.SMEM)


def cost(us):
    return pl.CostEstimate(flops=0, bytes_accessed=int(us * 3.69e6), transcendentals=0)


PARAMS = pltpu.CompilerParams(vmem_limit_bytes=60 * 1024 * 1024)
SMALL = pltpu.CompilerParams(vmem_limit_bytes=24 * 1024 * 1024)


def lanes(tile):
    return pl.ds(pl.multiple_of(tile * TILE, TILE), TILE)


def gather(x, index):
    return jnp.take_along_axis(x, index, axis=1, mode="promise_in_bounds")


def edges_kernel(dev_ref, first_ref, last_ref, list_ref, speed_ref, dir_ref, tab_ref,
                 low_ref, high_ref, wa_ref, wb_ref, mine_ref, other_ref, sems):
    copies = [
        pltpu.make_async_copy(tab_ref.at[dev_ref[0]], mine_ref, sems.at[0]),
        pltpu.make_async_copy(tab_ref.at[dev_ref[0] ^ 1], other_ref, sems.at[1]),
    ]
    for copy in copies:
        copy.start()
    for src, row, out in ((first_ref, 0, low_ref), (last_ref, 1, high_ref)):
        index = jnp.broadcast_to(list_ref[row : row + 1, :] & (TILE - 1), (PAD, TILE))
        out[...] = gather(src[...], index)
    speed, turn = speed_ref[...], dir_ref[...]
    wa_ref[...] = speed * jnp.cos(turn)
    wb_ref[...] = speed * jnp.sin(turn)
    for copy in copies:
        copy.wait()


def edges(dev, spectrum, send_list, wind_speed, wind_dir, tab):
    whole = lambda rows: pl.BlockSpec((rows, TILE), lambda i, d: (0, 0))
    shape = lambda rows: jax.ShapeDtypeStruct((rows, TILE), jnp.float32)
    return pl.pallas_call(
        edges_kernel,
        grid_spec=pltpu.PrefetchScalarGridSpec(
            num_scalar_prefetch=1,
            grid=(1,),
            in_specs=[
                pl.BlockSpec((PAD, TILE), lambda i, d: (0, 0)),
                pl.BlockSpec((PAD, TILE), lambda i, d: (0, NT - 1)),
                whole(2),
                whole(NT),
                whole(NT),
                pl.BlockSpec(memory_space=pltpu.HBM),
            ],
            out_specs=[whole(PAD)] * 2 + [whole(NT)] * 2 + [whole(PAD)] * 2,
            scratch_shapes=[pltpu.SemaphoreType.DMA((2,))],
        ),
        out_shape=[shape(PAD)] * 2 + [shape(NT)] * 2 + [shape(PAD)] * 2,
        compiler_params=PARAMS,
        cost_estimate=cost(0),
        name="edges",
    )(dev, spectrum, spectrum, send_list.reshape(2, TILE), wind_speed.reshape(NT, TILE), wind_dir.reshape(NT, TILE), tab)


GROUP = 8
GROUPS = NT // GROUP
SEGMENTS = 8
SEG_TILES = NT // SEGMENTS
MARGIN = GROUP + 1


def advect_kernel(last, base, tiles, *refs):
    if last:
        (dev_ref, counts_ref, state_ref, x_hbm, code_hbm, mask_hbm, wa_ref, wb_ref, tab_ref, lower_ref, upper_ref, order_ref,
         keep_ref, send_ref, par, dst, x_ref, code_ref, mask_ref, sems) = refs
    else:
        (dev_ref, counts_ref, x_hbm, code_hbm, mask_hbm, wa_ref, wb_ref, tab_ref, order_ref,
         keep_ref, send_ref, next_ref, par, dst, x_ref, code_ref, mask_ref, sems) = refs

    def copies(seg):
        at = pl.ds(pl.multiple_of(seg * (SEG_TILES * TILE), SEG_TILES * TILE), SEG_TILES * TILE)
        return (
            pltpu.make_async_copy(x_hbm.at[:, at], x_ref.at[:, at], sems.at[seg, 0]),
            pltpu.make_async_copy(code_hbm.at[:, at], code_ref.at[:, at], sems.at[seg, 1]),
            pltpu.make_async_copy(mask_hbm.at[:, at], mask_ref.at[:, at], sems.at[seg, 2]),
        )

    def start(seg, _):
        for copy in copies(seg):
            copy.start()
        return 0

    def wait(seg, _):
        for copy in copies(seg):
            copy.wait()
        return 0

    if last:
        g0, off0 = state_ref[0], state_ref[1]
        seg0 = jnp.maximum(g0 * GROUP - 1, 0) // SEG_TILES
    else:
        g0, off0, seg0 = jnp.int32(0), jnp.int32(0), jnp.int32(0)
    lax.fori_loop(seg0, SEGMENTS, start, 0)
    if last:
        edge = [
            pltpu.make_async_copy(x_hbm.at[:, pl.ds(0, 2 * TILE)], x_ref.at[:, pl.ds(NT * TILE, 2 * TILE)], sems.at[SEGMENTS, 0]),
            pltpu.make_async_copy(code_hbm.at[:, pl.ds(0, TILE)], code_ref.at[:, pl.ds(NT * TILE, TILE)], sems.at[SEGMENTS, 1]),
            pltpu.make_async_copy(mask_hbm.at[:, pl.ds(0, TILE)], mask_ref.at[:, pl.ds(NT * TILE, TILE)], sems.at[SEGMENTS, 2]),
        ]
        for copy in edge:
            copy.start()

    table = tab_ref[...]
    for i in range(7):
        par[i] = jnp.broadcast_to(table[:ROWS, i : i + 1], (ROWS, TILE))
    lane = lax.broadcasted_iota(jnp.int32, (ROWS, TILE), 1)

    def grown(t, at, before, after):
        own = x_ref[:, at]
        code = code_ref[:, at] & (TILE - 1)
        sea = mask_ref[:, at].astype(jnp.float32)
        to_east = par[5] > 0.5
        to_north = par[6] > 0.5
        near_x = gather(own, jnp.where(to_east, code[0:1], code[1:2]))
        near_x = near_x * jnp.where(to_east, sea[0:1], sea[1:2])
        near_y = gather(jnp.where(to_north, before, after), jnp.where(to_north, code[2:3], code[3:4]))
        near_y = near_y * jnp.where(to_north, sea[2:3], sea[3:4])
        value = own * par[4] + par[2] * near_x + par[3] * near_y
        drive = par[0] * wa_ref[pl.ds(t, 1), :] + par[1] * wb_ref[pl.ds(t, 1), :]
        return value * jnp.exp(jnp.maximum(drive - 0.08, 0.0))

    def store(value, off):
        shift = off & (TILE - 1)
        at = (off >> 7) - base + MARGIN
        dst[at] = jnp.where(lane < shift, dst[at], value)
        dst[at + 1] = value

    def step(g, off):
        values, offs = [], []
        for i in range(GROUP):
            t = g * GROUP + i
            before = x_ref[:, lanes(jnp.maximum(t - 1, 0))]
            after = x_ref[:, lanes(jnp.minimum(t + 1, NT - 1))]
            value = grown(t, lanes(t), before, after)
            values.append(pltpu.roll(value, off & (TILE - 1), 1))
            offs.append(off)
            inner = counts_ref[t]
            if i == 0:
                inner = jnp.where(g == 0, 0, inner)
            if i == GROUP - 1:
                inner = jnp.where(g == GROUPS - 1, 0, inner)
            off = off + inner
        for value, at in zip(values, offs):
            store(value, at)
        return off

    limit = (base + tiles) * TILE

    def body(c):
        g, off, _, ready = c
        need = jnp.minimum((g * GROUP + GROUP) // SEG_TILES, SEGMENTS - 1) + 1
        lax.fori_loop(ready, need, wait, 0)
        return g + 1, step(g, off), off, jnp.maximum(ready, need)

    if last:
        more = lambda c: c[0] < GROUPS
    else:
        total = lax.fori_loop(0, NT, lambda t, n: n + counts_ref[t], jnp.int32(0), unroll=8)
        share, rest = GROUPS * tiles // SEA_TILES, (SEA_TILES - tiles) * TILE
        more = lambda c: (c[0] < GROUPS) & (c[1] < limit) & ((c[0] < share) | (total - c[1] > rest))
    g, off, back, ready = lax.while_loop(
        more,
        body,
        (g0, off0, off0, seg0),
    )
    lax.fori_loop(ready, SEGMENTS, wait, 0)
    if last:
        for copy in edge:
            copy.wait()
        off = jnp.maximum(off, FIRST)
        value = grown(0, pl.ds(NT * TILE, TILE), lower_ref[:ROWS, :], x_ref[:, pl.ds((NT + 1) * TILE, TILE)])
        store(pltpu.roll(value, off & (TILE - 1), 1), off)
        off = off + counts_ref[0]
        value = grown(NT - 1, lanes(NT - 1), x_ref[:, lanes(NT - 2)], upper_ref[:ROWS, :])
        store(pltpu.roll(value, off & (TILE - 1), 1), off)
    else:
        straddles = off > limit
        next_ref[0] = jnp.where(straddles, g - 1, g)
        next_ref[1] = jnp.where(straddles, back, jnp.maximum(off, limit))
    half = tiles // 2
    core = dev_ref[0] & 1

    def emit(j, _):
        keep_ref[:ROWS, lanes(j)] = dst[MARGIN + core * half + j]
        send_ref[:ROWS, lanes(j)] = dst[MARGIN + (1 - core) * half + j]
        return 0

    lax.fori_loop(0, half, emit, 0, unroll=2)
    for out in (keep_ref, send_ref):
        out[ROWS:PAD, :] = jnp.zeros((PAD - ROWS, out.shape[1]), jnp.float32)


def advect(last, base, tiles, dev, counts, state, spectrum, codes, mask, wa, wb, tab, extra):
    half = tiles // 2 * TILE
    whole = lambda shape: pl.BlockSpec(shape, lambda i, d: (0,) * len(shape))
    hbm = pl.BlockSpec(memory_space=pltpu.HBM)
    tab_spec = whole((PAD, TILE))
    args = [counts] + ([state] if last else []) + [spectrum, codes, mask, wa, wb, tab] + extra
    specs = [SMEM] + ([SMEM] if last else [])
    specs += [hbm, hbm, hbm, whole((NT, TILE)), whole((NT, TILE)), tab_spec]
    specs += ([whole((PAD, TILE))] * 2 if last else []) + [pl.BlockSpec(memory_space=pl.ANY)]
    outs = [jax.ShapeDtypeStruct((PAD, half), jnp.float32)] * 2
    out_specs = [whole((PAD, half))] * 2
    if not last:
        outs = outs + [jax.ShapeDtypeStruct((2,), jnp.int32)]
        out_specs = out_specs + [SMEM]
    return pl.pallas_call(
        partial(advect_kernel, last, base, tiles),
        grid_spec=pltpu.PrefetchScalarGridSpec(
            num_scalar_prefetch=1,
            grid=(1,),
            in_specs=specs,
            out_specs=out_specs,
            scratch_shapes=[
                pltpu.VMEM((7, ROWS, TILE), jnp.float32),
                pltpu.VMEM((tiles + 2 * MARGIN + 2, ROWS, TILE), jnp.float32),
                pltpu.VMEM((ROWS, (NT + 2) * TILE), jnp.float32),
                pltpu.VMEM((4, (NT + 2) * TILE), jnp.int32),
                pltpu.VMEM((4, (NT + 2) * TILE), jnp.int32),
                pltpu.SemaphoreType.DMA((SEGMENTS + 1, 3)),
            ],
        ),
        out_shape=outs,
        compiler_params=PARAMS,
        cost_estimate=cost(0),
        name="advect",
    )(dev, *args)


def join_kernel(mine_ref, other_ref, tab_a, tab_b, *refs):
    both_ref, out_ref = refs[-2:]
    mine, other = mine_ref[...], other_ref[...]
    both_ref[:PAD] = mine
    both_ref[PAD:] = other
    fa, fb = tab_a[:, 7:8], tab_b[:, 7:8]
    out_ref[0:1, :] = jnp.sum(mine, axis=0, keepdims=True) + jnp.sum(other, axis=0, keepdims=True)
    out_ref[1:2, :] = jnp.sum(fa * mine, axis=0, keepdims=True) + jnp.sum(fb * other, axis=0, keepdims=True)


def join(mine, other, tabs, after=()):
    n = mine.shape[1]
    return pl.pallas_call(
        join_kernel,
        in_specs=[VMEM] * 4 + [pl.BlockSpec(memory_space=pl.ANY)] * len(after),
        out_specs=[VMEM] * 2,
        out_shape=[jax.ShapeDtypeStruct((2 * PAD, n), jnp.float32), jax.ShapeDtypeStruct((2, n), jnp.float32)],
        compiler_params=SMALL,
        cost_estimate=cost(0),
        name="join",
    )(mine, other, *tabs, *after)


def windows_kernel(*refs):
    tm, to, three_ref, two_ref = refs[-4:]

    def sums(mine, other, lane):
        fa, fb = tm[:, lane : lane + 1], to[:, lane : lane + 1]
        return (
            jnp.sum(mine, axis=0, keepdims=True) + jnp.sum(other, axis=0, keepdims=True),
            jnp.sum(fa * mine, axis=0, keepdims=True) + jnp.sum(fb * other, axis=0, keepdims=True),
        )

    at = 0
    for j in range(0, len(refs) - 4, 4):
        own, um, uo, down = refs[j : j + 4]
        n = own.shape[1]
        below = sums(um[...], uo[...], 8)
        above = sums(down[:PAD], down[PAD:], 9)
        for i in range(2):
            two = own[i : i + 1, :] + above[i]
            two_ref[i : i + 1, at : at + n] = two
            three_ref[i : i + 1, at : at + n] = two + below[i]
        at += n


def moment_windows(chunks, tabs):
    args = [x for own, up, down in chunks for x in (own, *up, down)]
    total = sum(own.shape[1] for own, _, _ in chunks)
    return pl.pallas_call(
        windows_kernel,
        in_specs=[VMEM] * (len(args) + 2),
        out_specs=[VMEM] * 2,
        out_shape=[jax.ShapeDtypeStruct((2, total), jnp.float32)] * 2,
        compiler_params=SMALL,
        cost_estimate=cost(0),
        name="moment_windows",
    )(*args, *tabs)


def far_kernel(dev_ref, *refs):
    out_ref = refs[-1]
    core = dev_ref[0] & 1
    turn = ((dev_ref[0] >> 1) - 1) & 3

    def fill(parts):
        at = 0
        for low in parts:
            n = low.shape[1]
            out_ref[0:3, at : at + n] = jnp.where(turn == 1, low[9:12, :], low[3:6, :])
            out_ref[3:4, at : at + n] = jnp.zeros((1, n), jnp.float32)
            at += n

    @pl.when(core == 0)
    def _():
        fill(refs[0:-1:2])

    @pl.when(core == 1)
    def _():
        fill(refs[1:-1:2])


def far_pack(dev, *pairs):
    total = sum(p[0].shape[1] for p in pairs)
    whole = lambda shape: pl.BlockSpec(shape, lambda i, d: (0, 0))
    return pl.pallas_call(
        far_kernel,
        grid_spec=pltpu.PrefetchScalarGridSpec(
            num_scalar_prefetch=1,
            grid=(1,),
            in_specs=[whole((16, x.shape[1])) for pair in pairs for x in pair],
            out_specs=whole((FAR, total)),
        ),
        out_shape=jax.ShapeDtypeStruct((FAR, total), jnp.float32),
        compiler_params=SMALL,
        cost_estimate=cost(0),
        name="far_pack",
    )(dev, *[x for pair in pairs for x in pair])


def relay_kernel(dev_ref, mine_ref, other_ref, *refs):
    out_ref = refs[-1]
    core = dev_ref[0] & 1
    turn = ((dev_ref[0] >> 1) + 1) & 3

    def fill(rows):
        row = lambda i: rows[i : i + 1, :]
        out_ref[...] = rows[16:40, :]
        out_ref[0:1, :] = jnp.where(turn == 1, row(15), jnp.where(turn == 2, row(9), row(3)))

    @pl.when(core == 1)
    def _():
        fill(mine_ref)

    @pl.when(core == 0)
    def _():
        fill(other_ref)


def relay_pack(dev, up, after=()):
    n = up[0].shape[1]
    return pl.pallas_call(
        relay_kernel,
        grid_spec=pltpu.PrefetchScalarGridSpec(
            num_scalar_prefetch=1,
            grid=(1,),
            in_specs=[pl.BlockSpec(x.shape, lambda i, d: (0, 0)) for x in up]
            + [pl.BlockSpec(memory_space=pl.ANY)] * len(after),
            out_specs=pl.BlockSpec((RELAY, n), lambda i, d: (0, 0)),
        ),
        out_shape=jax.ShapeDtypeStruct((RELAY, n), jnp.float32),
        compiler_params=SMALL,
        cost_estimate=cost(0),
        name="relay_pack",
    )(dev, *up, *after)


def sources_kernel(dev_ref, w_ref, tab_a, tab_b, sum_a, sum_b, sum_c, *refs):
    pieces, (mine_out, other_out) = refs[:-2], refs[-2:]
    far = pieces[-1][...]
    stacked_in = jnp.concatenate([p[...] for p in pieces[:-1]] + [far, jnp.zeros_like(far)], axis=0)
    high = stacked_in.astype(jnp.bfloat16)
    low = (stacked_in - high.astype(jnp.float32)).astype(jnp.bfloat16)
    stacked = jnp.concatenate([high, high, low], axis=0)
    shifted = jnp.dot(w_ref[0], stacked, preferred_element_type=jnp.float32)
    energy_sum = (sum_a[0:1, :] + sum_b[0:1, :] + sum_c[0:1, :]) * (1.0 / K) + EPS
    first_moment = ((sum_a[1:2, :] + sum_b[1:2, :] + sum_c[1:2, :]) * (1.0 / K) + EPS * MEAN_FREQ) / energy_sum
    ratio = first_moment * (1.0 / MEAN_FREQ)
    ratio = ratio * ratio
    steepness = energy_sum * (ratio * ratio)
    inverse = 1.0 / first_moment
    fade = -0.3 * inverse * (steepness * steepness)
    gain = 0.05 * inverse
    cross = 2.0 * CROSS_FACTOR / (PLUS_FACTOR * MINUS_FACTOR)
    for at, tab, out in ((0, tab_a, mine_out), (PAD, tab_b, other_out)):
        freq = tab[:, 7:8]
        g = stacked_in[at : at + PAD]
        upper = shifted[at : at + PAD]
        lower = shifted[2 * PAD + at : 2 * PAD + at + PAD]
        out[...] = g * (jnp.exp(freq * fade) + (freq * gain) * (g * (upper + lower) - cross * (upper * lower)))


def sources(dev, weights, tabs, sums, pieces, far, start):
    n = pieces[0].shape[1]
    block = BLOCK
    skip = start // block
    spec = lambda rows: pl.BlockSpec((rows, block), lambda i, d: (0, i))
    wide = lambda rows: pl.BlockSpec((rows, block), lambda i, d: (0, i + skip))
    return pl.pallas_call(
        sources_kernel,
        grid_spec=pltpu.PrefetchScalarGridSpec(
            num_scalar_prefetch=1,
            grid=(n // block,),
            in_specs=[pl.BlockSpec((1, 4 * PAD, 3 * PIECES), lambda i, d: (d[0], 0, 0))]
            + [pl.BlockSpec((PAD, TILE), lambda i, d: (0, 0))] * 2
            + [wide(2)] * 3
            + [spec(p.shape[0]) for p in pieces]
            + [wide(FAR)],
            out_specs=[spec(PAD)] * 2,
        ),
        out_shape=[jax.ShapeDtypeStruct((PAD, n), jnp.float32)] * 2,
        compiler_params=SMALL,
        cost_estimate=cost(0),
        name="sources",
    )(dev, weights, *tabs, *sums, *pieces, far)


def expand_kernel(dev_ref, counts_ref, state_ref, *refs):
    count = 2 * len(CHUNKS)
    pieces = refs[:count]
    out_ref, held, room, sems = refs[count:]
    core = dev_ref[0] & 1
    base = 0
    for i, tiles in enumerate(CHUNKS):
        half = tiles // 2
        mine, other = pieces[2 * i], pieces[2 * i + 1]

        def fill(j, _, mine=mine, other=other, base=base, half=half):
            held[base + core * half + j] = mine[:, lanes(j)]
            held[base + (1 - core) * half + j] = other[:, lanes(j)]
            return 0

        lax.fori_loop(0, half, fill, 0, unroll=2)
        base += tiles
    lane = lax.broadcasted_iota(jnp.int32, (PAD, TILE), 1)

    def placed(t, off):
        shift = off & (TILE - 1)
        at = off >> 7
        value = jnp.where(lane >= shift, held[at], held[at + 1])
        value = pltpu.roll(value, (TILE - shift) & (TILE - 1), 1)
        return jnp.where(lane < counts_ref[t], value, 0.0)

    def copy(seg):
        at = pl.ds(pl.multiple_of(seg * (SEG_TILES * TILE), SEG_TILES * TILE), SEG_TILES * TILE)
        return pltpu.make_async_copy(room.at[:, at], out_ref.at[:, at], sems.at[seg])

    def step(g, off):
        values = []
        off = jnp.where(g == state_ref[0], state_ref[1], off)
        for i in range(GROUP):
            t = g * GROUP + i
            values.append(placed(t, off))
            inner = counts_ref[t]
            if i == 0:
                inner = jnp.where(g == 0, 0, inner)
            if i == GROUP - 1:
                inner = jnp.where(g == GROUPS - 1, 0, inner)
            off = off + inner
        for i, value in enumerate(values):
            room[:, lanes(g * GROUP + i)] = value[:ROWS]
        return off

    per = SEG_TILES // GROUP

    def segment(seg, off):
        off = lax.fori_loop(seg * per, seg * per + per, step, off)

        @pl.when((seg > 0) & (seg < SEGMENTS - 1))
        def _():
            copy(seg).start()

        return off

    off = lax.fori_loop(0, SEGMENTS, segment, jnp.int32(0))
    off = jnp.maximum(off, FIRST)
    room[:, lanes(0)] = placed(0, off)[:ROWS]
    copy(0).start()
    off = off + counts_ref[0]
    room[:, lanes(NT - 1)] = placed(NT - 1, off)[:ROWS]
    copy(SEGMENTS - 1).start()
    for seg in range(SEGMENTS):
        copy(seg).wait()


def expand(dev, counts, state, pieces):
    whole = lambda shape: pl.BlockSpec(shape, lambda i, d: (0,) * len(shape))
    return pl.pallas_call(
        expand_kernel,
        grid_spec=pltpu.PrefetchScalarGridSpec(
            num_scalar_prefetch=1,
            grid=(1,),
            in_specs=[SMEM, SMEM] + [whole(p.shape) for p in pieces],
            out_specs=pl.BlockSpec(memory_space=pltpu.HBM),
            scratch_shapes=[
                pltpu.VMEM((SEA_TILES + 4, PAD, TILE), jnp.float32),
                pltpu.VMEM((ROWS, NT * TILE), jnp.float32),
                pltpu.SemaphoreType.DMA((SEGMENTS,)),
            ],
        ),
        out_shape=jax.ShapeDtypeStruct((ROWS, NT * TILE), jnp.float32),
        compiler_params=SMALL,
        cost_estimate=cost(0),
        name="expand",
    )(dev, counts, state, *pieces)


def per_device(spectrum, wind_speed, wind_dir, counts, send_list, neighbors, neighbor_mask):
    dev = lax.axis_index("spec").astype(jnp.int32).reshape(1)
    tab = jnp.asarray(component_params())
    weights = jnp.asarray(interaction_weights())

    def shift(x, hops):
        return lax.ppermute(x, "spec", [(s, (s + hops) % N_SPEC) for s in range(N_SPEC)])

    def cross(x, hops):
        return lax.ppermute(x, "spec", [(s, ((s + hops) % N_SPEC) ^ 1) for s in range(N_SPEC)])

    def swap(x):
        return lax.ppermute(x, "spec", [(s, s ^ 1) for s in range(N_SPEC)])

    to_lower, to_upper, wa, wb, *tabs = edges(dev, spectrum, send_list, wind_speed, wind_dir, tab)
    lower = lax.ppermute(to_upper, "space", [(s, (s + 1) % N_SPACE) for s in range(N_SPACE)])
    upper = lax.ppermute(to_lower, "space", [(s, (s - 1) % N_SPACE) for s in range(N_SPACE)])

    mine, send, state = advect(
        False, 0, CHUNKS[0], dev, counts, None, spectrum, neighbors, neighbor_mask, wa, wb, tabs[0], [wa]
    )
    up1 = shift(mine, 2), cross(send, 2)
    own1 = mine, swap(send)
    both1, sums1 = join(*own1, tabs)
    down1 = shift(both1, -2)
    mine, send = advect(
        True, CHUNKS[0], CHUNKS[1], dev, counts, state, spectrum, neighbors, neighbor_mask, wa, wb, tabs[0],
        [lower, upper, sums1],
    )
    up2 = shift(mine, 2), cross(send, 2)
    own2 = mine, swap(send)
    both2, sums2 = join(*own2, tabs, up1)
    down2 = shift(both2, -2)
    far = shift(far_pack(dev, own1, own2), -4)
    three, two = moment_windows([(sums1, up1, down1), (sums2, up2, down2)], tabs)
    sums = three, shift(three, -6), shift(two, 6)
    relay1 = shift(relay_pack(dev, up1), 2)
    relay2 = shift(relay_pack(dev, up2, [far, three]), 2)
    results, start = [], 0
    for pieces in ([both1, *up1, down1, relay1], [both2, *up2, down2, relay2]):
        mine, other = sources(dev, weights, tabs, sums, pieces, far, start)
        start += mine.shape[1]
        results += [mine, swap(other)]
    return expand(dev, counts, state, results)


def solution(mesh):
    in_specs = (
        P("spec", "space"),
        P("space"),
        P("space"),
        P("space"),
        P("space"),
        P(None, "space"),
        P(None, "space"),
    )
    out_specs = P("spec", "space")
    return jax.shard_map(
        per_device, mesh=mesh, in_specs=in_specs, out_specs=out_specs, check_vma=False
    )
```

```python
import math
from functools import partial

import jax
import jax.numpy as jnp
import ml_dtypes
import numpy as np
from jax import lax
from jax.experimental import pallas as pl
from jax.experimental.pallas import tpu as pltpu
from jax.sharding import PartitionSpec as P

ND = 24
NF = 26
TILE = 128
K = 624
NT = 128
ROWS = 39
PAD = 40
CHIPS = 8
CHIP_ROWS = 78
N_SPACE = 16
N_SPEC = 16

LOG_RATIO = math.log(1.1)
FREQ_LOW = 0.05
EPS = 1e-06
PLUS_FACTOR = 1.0 / 1.25**4
MINUS_FACTOR = 1.0 / 0.75**4
CROSS_FACTOR = 1.0 / 0.9375**4

CHUNKS = (40, 40)
FIRST = CHUNKS[0] * TILE
SEA_TILES = sum(CHUNKS)
BLOCK = 1280

RELAY = 24
FAR = 4
PIECES = 6 * PAD + RELAY + 8


def tables():
    k = np.arange(K)
    level = (k // ND).astype(np.float64)
    heading = ((k % ND) + 0.5) * (2.0 * math.pi / ND)
    frequency = FREQ_LOW * np.exp(LOG_RATIO * level)
    courant = 0.6 * np.exp(-LOG_RATIO * level)
    return frequency, heading, courant


FREQ = tables()[0]
MEAN_FREQ = float(FREQ.mean())


def component_params():
    frequency, heading, courant = tables()
    east = courant * np.cos(heading)
    north = courant * np.sin(heading)
    cols = (
        0.08 * frequency * np.cos(heading) / 1.56,
        0.08 * frequency * np.sin(heading) / 1.56,
        np.abs(east),
        np.abs(north),
        1.0 - np.abs(east) - np.abs(north),
        (east > 0).astype(np.float64),
        (north > 0).astype(np.float64),
        frequency,
    )
    out = np.zeros((N_SPEC, PAD, TILE), np.float32)
    for lane, col in enumerate(cols):
        out[:, :ROWS, lane] = col.reshape(N_SPEC, ROWS)
    out[:, :, 8] = np.roll(out[:, :, 7], 2, axis=0)
    out[:, :, 9] = np.roll(out[:, :, 7], -2, axis=0)
    return out


def interaction_table(dir_count, freq_count):
    comp_total = dir_count * freq_count
    matrix = np.zeros((2 * comp_total, comp_total), np.float32)
    shifts = (
        (math.log(1.25) / math.log(1.1), 33.56 * dir_count / 360.0),
        (math.log(0.75) / math.log(1.1), 11.48 * dir_count / 360.0),
    )
    for which_half, (band_shift, turning) in enumerate(shifts):
        for band_level in range(freq_count):
            band_place = band_level + band_shift
            low_band = math.floor(band_place)
            frac_band = band_place - low_band
            for mirror in (1.0, -1.0):
                for heading in range(dir_count):
                    dir_place = heading + mirror * turning
                    low_dir = math.floor(dir_place)
                    frac_dir = dir_place - low_dir
                    row_index = which_half * comp_total + band_level * dir_count + heading
                    for band_step, band_weight in ((0, 1.0 - frac_band), (1, frac_band)):
                        source_band = low_band + band_step
                        if 0 <= source_band < freq_count:
                            for dir_step, dir_weight in ((0, 1.0 - frac_dir), (1, frac_dir)):
                                source_dir = (low_dir + dir_step) % dir_count
                                matrix[row_index, source_band * dir_count + source_dir] += (
                                    0.5 * band_weight * dir_weight
                                )
    return matrix


def piece_columns(dev):
    chip, core = divmod(dev, 2)

    def rows(offset, which):
        first = ((chip + offset) % CHIPS) * CHIP_ROWS + ROWS * which
        return list(range(first, first + ROWS)) + [-1]

    cols = []
    for offset in (0, -1, 1):
        cols += rows(offset, core) + rows(offset, 1 - core)
    below = rows(-2, 1)
    turn = 6 * (chip % 4)
    cols += [below[21 - turn] if turn else -1, -1, -1, -1] + below[20:40]
    above = rows(2, 0)
    turn = 6 * ((chip + 1) % 4)
    cols += (above[9:12] if turn == 6 else above[3:6] if turn == 12 else [-1] * 3) + [-1] * 5
    return cols


def interaction_weights():
    table = interaction_table(ND, NF)
    out = np.zeros((N_SPEC, 4 * PAD, PIECES), np.float32)
    for dev in range(N_SPEC):
        cols = np.array(piece_columns(dev))
        held = cols[cols >= 0]
        assert len(cols) == PIECES and len(set(held.tolist())) == len(held)
        for half, factor in ((0, PLUS_FACTOR), (1, MINUS_FACTOR)):
            for slot, owner in enumerate((dev, dev ^ 1)):
                want = table[half * K + ROWS * owner : half * K + ROWS * owner + ROWS]
                got = np.where(cols >= 0, want[:, np.maximum(cols, 0)], 0.0)
                assert np.array_equal((got != 0).sum(1), (want != 0).sum(1))
                at = half * 2 * PAD + slot * PAD
                out[dev, at : at + ROWS] = got * factor
    high = out.astype(ml_dtypes.bfloat16)
    low = (out - high.astype(np.float32)).astype(ml_dtypes.bfloat16)
    return np.concatenate([high, low, high], axis=2)


VMEM = pl.BlockSpec(memory_space=pltpu.VMEM)
SMEM = pl.BlockSpec(memory_space=pltpu.SMEM)


def cost(us):
    return pl.CostEstimate(flops=0, bytes_accessed=int(us * 3.69e6), transcendentals=0)


PARAMS = pltpu.CompilerParams(vmem_limit_bytes=60 * 1024 * 1024)
SMALL = pltpu.CompilerParams(vmem_limit_bytes=24 * 1024 * 1024)


def lanes(tile):
    return pl.ds(pl.multiple_of(tile * TILE, TILE), TILE)


def gather(x, index):
    return jnp.take_along_axis(x, index, axis=1, mode="promise_in_bounds")


def edges_kernel(dev_ref, first_ref, last_ref, list_ref, speed_ref, dir_ref, tab_ref,
                 low_ref, high_ref, wa_ref, wb_ref, mine_ref, other_ref, sems):
    copies = [
        pltpu.make_async_copy(tab_ref.at[dev_ref[0]], mine_ref, sems.at[0]),
        pltpu.make_async_copy(tab_ref.at[dev_ref[0] ^ 1], other_ref, sems.at[1]),
    ]
    for copy in copies:
        copy.start()
    for src, row, out in ((first_ref, 0, low_ref), (last_ref, 1, high_ref)):
        index = jnp.broadcast_to(list_ref[row : row + 1, :] & (TILE - 1), (PAD, TILE))
        out[...] = gather(src[...], index)
    speed, turn = speed_ref[...], dir_ref[...]
    wa_ref[...] = speed * jnp.cos(turn)
    wb_ref[...] = speed * jnp.sin(turn)
    for copy in copies:
        copy.wait()


def edges(dev, spectrum, send_list, wind_speed, wind_dir, tab):
    whole = lambda rows: pl.BlockSpec((rows, TILE), lambda i, d: (0, 0))
    shape = lambda rows: jax.ShapeDtypeStruct((rows, TILE), jnp.float32)
    return pl.pallas_call(
        edges_kernel,
        grid_spec=pltpu.PrefetchScalarGridSpec(
            num_scalar_prefetch=1,
            grid=(1,),
            in_specs=[
                pl.BlockSpec((PAD, TILE), lambda i, d: (0, 0)),
                pl.BlockSpec((PAD, TILE), lambda i, d: (0, NT - 1)),
                whole(2),
                whole(NT),
                whole(NT),
                pl.BlockSpec(memory_space=pltpu.HBM),
            ],
            out_specs=[whole(PAD)] * 2 + [whole(NT)] * 2 + [whole(PAD)] * 2,
            scratch_shapes=[pltpu.SemaphoreType.DMA((2,))],
        ),
        out_shape=[shape(PAD)] * 2 + [shape(NT)] * 2 + [shape(PAD)] * 2,
        compiler_params=PARAMS,
        cost_estimate=cost(0),
        name="edges",
    )(dev, spectrum, spectrum, send_list.reshape(2, TILE), wind_speed.reshape(NT, TILE), wind_dir.reshape(NT, TILE), tab)


GROUP = 8
GROUPS = NT // GROUP
SEGMENTS = 8
SEG_TILES = NT // SEGMENTS
MARGIN = GROUP + 1


def advect_kernel(last, base, tiles, *refs):
    if last:
        (dev_ref, counts_ref, state_ref, x_hbm, code_hbm, mask_hbm, wa_ref, wb_ref, tab_ref, lower_ref, upper_ref, order_ref,
         both_ref, send_ref, par, dst, x_ref, code_ref, mask_ref, sems) = refs
    else:
        (dev_ref, counts_ref, x_hbm, code_hbm, mask_hbm, wa_ref, wb_ref, tab_ref, order_ref,
         both_ref, send_ref, next_ref, par, dst, x_ref, code_ref, mask_ref, sems) = refs

    def copies(seg):
        at = pl.ds(pl.multiple_of(seg * (SEG_TILES * TILE), SEG_TILES * TILE), SEG_TILES * TILE)
        return (
            pltpu.make_async_copy(x_hbm.at[:, at], x_ref.at[:, at], sems.at[seg, 0]),
            pltpu.make_async_copy(code_hbm.at[:, at], code_ref.at[:, at], sems.at[seg, 1]),
            pltpu.make_async_copy(mask_hbm.at[:, at], mask_ref.at[:, at], sems.at[seg, 2]),
        )

    def start(seg, _):
        for copy in copies(seg):
            copy.start()
        return 0

    def wait(seg, _):
        for copy in copies(seg):
            copy.wait()
        return 0

    if last:
        g0, off0 = state_ref[0], state_ref[1]
        seg0 = jnp.maximum(g0 * GROUP - 1, 0) // SEG_TILES
    else:
        g0, off0, seg0 = jnp.int32(0), jnp.int32(0), jnp.int32(0)
    lax.fori_loop(seg0, SEGMENTS, start, 0)
    if last:
        edge = [
            pltpu.make_async_copy(x_hbm.at[:, pl.ds(0, 2 * TILE)], x_ref.at[:, pl.ds(NT * TILE, 2 * TILE)], sems.at[SEGMENTS, 0]),
            pltpu.make_async_copy(code_hbm.at[:, pl.ds(0, TILE)], code_ref.at[:, pl.ds(NT * TILE, TILE)], sems.at[SEGMENTS, 1]),
            pltpu.make_async_copy(mask_hbm.at[:, pl.ds(0, TILE)], mask_ref.at[:, pl.ds(NT * TILE, TILE)], sems.at[SEGMENTS, 2]),
        ]
        for copy in edge:
            copy.start()

    table = tab_ref[...]
    for i in range(7):
        par[i] = jnp.broadcast_to(table[:ROWS, i : i + 1], (ROWS, TILE))
    lane = lax.broadcasted_iota(jnp.int32, (ROWS, TILE), 1)

    def grown(t, at, before, after):
        own = x_ref[:, at]
        code = code_ref[:, at] & (TILE - 1)
        sea = mask_ref[:, at].astype(jnp.float32)
        to_east = par[5] > 0.5
        to_north = par[6] > 0.5
        near_x = gather(own, jnp.where(to_east, code[0:1], code[1:2]))
        near_x = near_x * jnp.where(to_east, sea[0:1], sea[1:2])
        near_y = gather(jnp.where(to_north, before, after), jnp.where(to_north, code[2:3], code[3:4]))
        near_y = near_y * jnp.where(to_north, sea[2:3], sea[3:4])
        value = own * par[4] + par[2] * near_x + par[3] * near_y
        drive = par[0] * wa_ref[pl.ds(t, 1), :] + par[1] * wb_ref[pl.ds(t, 1), :]
        return value * jnp.exp(jnp.maximum(drive - 0.08, 0.0))

    def store(value, off):
        shift = off & (TILE - 1)
        at = (off >> 7) - base + MARGIN
        dst[at] = jnp.where(lane < shift, dst[at], value)
        dst[at + 1] = value

    def step(g, off):
        values, offs = [], []
        for i in range(GROUP):
            t = g * GROUP + i
            before = x_ref[:, lanes(jnp.maximum(t - 1, 0))]
            after = x_ref[:, lanes(jnp.minimum(t + 1, NT - 1))]
            value = grown(t, lanes(t), before, after)
            values.append(pltpu.roll(value, off & (TILE - 1), 1))
            offs.append(off)
            inner = counts_ref[t]
            if i == 0:
                inner = jnp.where(g == 0, 0, inner)
            if i == GROUP - 1:
                inner = jnp.where(g == GROUPS - 1, 0, inner)
            off = off + inner
        for value, at in zip(values, offs):
            store(value, at)
        return off

    limit = (base + tiles) * TILE

    def body(c):
        g, off, _, ready = c
        need = jnp.minimum((g * GROUP + GROUP) // SEG_TILES, SEGMENTS - 1) + 1
        lax.fori_loop(ready, need, wait, 0)
        return g + 1, step(g, off), off, jnp.maximum(ready, need)

    if last:
        more = lambda c: c[0] < GROUPS
    else:
        total = lax.fori_loop(0, NT, lambda t, n: n + counts_ref[t], jnp.int32(0), unroll=8)
        share, rest = GROUPS * tiles // SEA_TILES, (SEA_TILES - tiles) * TILE
        more = lambda c: (c[0] < GROUPS) & (c[1] < limit) & ((c[0] < share) | (total - c[1] > rest))
    g, off, back, ready = lax.while_loop(
        more,
        body,
        (g0, off0, off0, seg0),
    )
    lax.fori_loop(ready, SEGMENTS, wait, 0)
    if last:
        for copy in edge:
            copy.wait()
        off = jnp.maximum(off, FIRST)
        value = grown(0, pl.ds(NT * TILE, TILE), lower_ref[:ROWS, :], x_ref[:, pl.ds((NT + 1) * TILE, TILE)])
        store(pltpu.roll(value, off & (TILE - 1), 1), off)
        off = off + counts_ref[0]
        value = grown(NT - 1, lanes(NT - 1), x_ref[:, lanes(NT - 2)], upper_ref[:ROWS, :])
        store(pltpu.roll(value, off & (TILE - 1), 1), off)
    else:
        straddles = off > limit
        next_ref[0] = jnp.where(straddles, g - 1, g)
        next_ref[1] = jnp.where(straddles, back, jnp.maximum(off, limit))
    half = tiles // 2
    core = dev_ref[0] & 1

    def emit(j, _):
        other = dst[MARGIN + (1 - core) * half + j]
        both_ref[:ROWS, lanes(j)] = dst[MARGIN + core * half + j]
        both_ref[PAD : PAD + ROWS, lanes(j)] = other
        send_ref[:ROWS, lanes(j)] = other
        return 0

    lax.fori_loop(0, half, emit, 0, unroll=2)
    none = jnp.zeros((PAD - ROWS, send_ref.shape[1]), jnp.float32)
    both_ref[ROWS:PAD, :] = none
    both_ref[PAD + ROWS :, :] = none
    send_ref[ROWS:, :] = none


def advect(last, base, tiles, dev, counts, state, spectrum, codes, mask, wa, wb, tab, extra):
    half = tiles // 2 * TILE
    whole = lambda shape: pl.BlockSpec(shape, lambda i, d: (0,) * len(shape))
    hbm = pl.BlockSpec(memory_space=pltpu.HBM)
    tab_spec = whole((PAD, TILE))
    args = [counts] + ([state] if last else []) + [spectrum, codes, mask, wa, wb, tab] + extra
    specs = [SMEM] + ([SMEM] if last else [])
    specs += [hbm, hbm, hbm, whole((NT, TILE)), whole((NT, TILE)), tab_spec]
    specs += ([whole((PAD, TILE))] * 2 if last else []) + [pl.BlockSpec(memory_space=pl.ANY)]
    outs = [jax.ShapeDtypeStruct((rows, half), jnp.float32) for rows in (2 * PAD, PAD)]
    out_specs = [whole((rows, half)) for rows in (2 * PAD, PAD)]
    if not last:
        outs = outs + [jax.ShapeDtypeStruct((2,), jnp.int32)]
        out_specs = out_specs + [SMEM]
    return pl.pallas_call(
        partial(advect_kernel, last, base, tiles),
        grid_spec=pltpu.PrefetchScalarGridSpec(
            num_scalar_prefetch=1,
            grid=(1,),
            in_specs=specs,
            out_specs=out_specs,
            scratch_shapes=[
                pltpu.VMEM((7, ROWS, TILE), jnp.float32),
                pltpu.VMEM((tiles + 2 * MARGIN + 2, ROWS, TILE), jnp.float32),
                pltpu.VMEM((ROWS, (NT + 2) * TILE), jnp.float32),
                pltpu.VMEM((4, (NT + 2) * TILE), jnp.int32),
                pltpu.VMEM((4, (NT + 2) * TILE), jnp.int32),
                pltpu.SemaphoreType.DMA((SEGMENTS + 1, 3)),
            ],
        ),
        out_shape=outs,
        compiler_params=PARAMS,
        cost_estimate=cost(0),
        name="advect",
    )(dev, *args)


def head(x):
    return pl.BlockSpec((PAD, x.shape[1]), lambda *i: (0, 0))


def moments_kernel(mine_ref, other_ref, tab_a, tab_b, out_ref):
    mine, other = mine_ref[...], other_ref[...]
    fa, fb = tab_a[:, 7:8], tab_b[:, 7:8]
    out_ref[0:1, :] = jnp.sum(mine, axis=0, keepdims=True) + jnp.sum(other, axis=0, keepdims=True)
    out_ref[1:2, :] = jnp.sum(fa * mine, axis=0, keepdims=True) + jnp.sum(fb * other, axis=0, keepdims=True)


def moments(mine, other, tabs):
    n = mine.shape[1]
    return pl.pallas_call(
        moments_kernel,
        grid=(1,),
        in_specs=[head(mine), head(other)] + [pl.BlockSpec((PAD, TILE), lambda i: (0, 0))] * 2,
        out_specs=pl.BlockSpec((2, n), lambda i: (0, 0)),
        out_shape=jax.ShapeDtypeStruct((2, n), jnp.float32),
        compiler_params=SMALL,
        cost_estimate=cost(0),
        name="moments",
    )(mine, other, *tabs)


def windows_kernel(*refs):
    tm, to, three_ref, two_ref = refs[-4:]

    def sums(mine, other, lane):
        fa, fb = tm[:, lane : lane + 1], to[:, lane : lane + 1]
        return (
            jnp.sum(mine, axis=0, keepdims=True) + jnp.sum(other, axis=0, keepdims=True),
            jnp.sum(fa * mine, axis=0, keepdims=True) + jnp.sum(fb * other, axis=0, keepdims=True),
        )

    at = 0
    for j in range(0, len(refs) - 4, 5):
        own, um, uo, dm, do = refs[j : j + 5]
        n = own.shape[1]
        below = sums(um[...], uo[...], 8)
        above = sums(dm[...], do[...], 9)
        for i in range(2):
            two = own[i : i + 1, :] + above[i]
            two_ref[i : i + 1, at : at + n] = two
            three_ref[i : i + 1, at : at + n] = two + below[i]
        at += n


def moment_windows(chunks, tabs):
    args = [x for own, up, down in chunks for x in (own, *up, *down)]
    total = sum(own.shape[1] for own, _, _ in chunks)
    return pl.pallas_call(
        windows_kernel,
        grid=(1,),
        in_specs=[head(x) if x.shape[0] > 2 else pl.BlockSpec(x.shape, lambda i: (0, 0)) for x in args]
        + [pl.BlockSpec((PAD, TILE), lambda i: (0, 0))] * 2,
        out_specs=[pl.BlockSpec((2, total), lambda i: (0, 0))] * 2,
        out_shape=[jax.ShapeDtypeStruct((2, total), jnp.float32)] * 2,
        compiler_params=SMALL,
        cost_estimate=cost(0),
        name="moment_windows",
    )(*args, *tabs)


def far_kernel(dev_ref, *refs):
    out_ref = refs[-1]
    core = dev_ref[0] & 1
    turn = ((dev_ref[0] >> 1) - 1) & 3

    def fill(parts):
        at = 0
        for low in parts:
            n = low.shape[1]
            out_ref[0:3, at : at + n] = jnp.where(turn == 1, low[9:12, :], low[3:6, :])
            out_ref[3:4, at : at + n] = jnp.zeros((1, n), jnp.float32)
            at += n

    @pl.when(core == 0)
    def _():
        fill(refs[0:-1:2])

    @pl.when(core == 1)
    def _():
        fill(refs[1:-1:2])


def far_pack(dev, *pairs):
    total = sum(p[0].shape[1] for p in pairs)
    whole = lambda shape: pl.BlockSpec(shape, lambda i, d: (0, 0))
    return pl.pallas_call(
        far_kernel,
        grid_spec=pltpu.PrefetchScalarGridSpec(
            num_scalar_prefetch=1,
            grid=(1,),
            in_specs=[whole((16, x.shape[1])) for pair in pairs for x in pair],
            out_specs=whole((FAR, total)),
        ),
        out_shape=jax.ShapeDtypeStruct((FAR, total), jnp.float32),
        compiler_params=SMALL,
        cost_estimate=cost(0),
        name="far_pack",
    )(dev, *[x for pair in pairs for x in pair])


def relay_kernel(dev_ref, mine_ref, other_ref, *refs):
    out_ref = refs[-1]
    core = dev_ref[0] & 1
    turn = ((dev_ref[0] >> 1) + 1) & 3

    def fill(rows):
        row = lambda i: rows[i : i + 1, :]
        out_ref[...] = rows[16:40, :]
        out_ref[0:1, :] = jnp.where(turn == 1, row(15), jnp.where(turn == 2, row(9), row(3)))

    @pl.when(core == 1)
    def _():
        fill(mine_ref)

    @pl.when(core == 0)
    def _():
        fill(other_ref)


def relay_pack(dev, up, after=()):
    n = up[0].shape[1]
    return pl.pallas_call(
        relay_kernel,
        grid_spec=pltpu.PrefetchScalarGridSpec(
            num_scalar_prefetch=1,
            grid=(1,),
            in_specs=[head(x) for x in up]
            + [pl.BlockSpec(memory_space=pl.ANY)] * len(after),
            out_specs=pl.BlockSpec((RELAY, n), lambda i, d: (0, 0)),
        ),
        out_shape=jax.ShapeDtypeStruct((RELAY, n), jnp.float32),
        compiler_params=SMALL,
        cost_estimate=cost(0),
        name="relay_pack",
    )(dev, *up, *after)


def sources_kernel(dev_ref, w_ref, tab_a, tab_b, sum_a, sum_b, sum_c, *refs):
    pieces, (mine_out, other_out) = refs[:-2], refs[-2:]
    far = pieces[-1][...]
    stacked_in = jnp.concatenate([p[...] for p in pieces[:-1]] + [far, jnp.zeros_like(far)], axis=0)
    high = stacked_in.astype(jnp.bfloat16)
    low = (stacked_in - high.astype(jnp.float32)).astype(jnp.bfloat16)
    stacked = jnp.concatenate([high, high, low], axis=0)
    shifted = jnp.dot(w_ref[0], stacked, preferred_element_type=jnp.float32)
    energy_sum = (sum_a[0:1, :] + sum_b[0:1, :] + sum_c[0:1, :]) * (1.0 / K) + EPS
    first_moment = ((sum_a[1:2, :] + sum_b[1:2, :] + sum_c[1:2, :]) * (1.0 / K) + EPS * MEAN_FREQ) / energy_sum
    ratio = first_moment * (1.0 / MEAN_FREQ)
    ratio = ratio * ratio
    steepness = energy_sum * (ratio * ratio)
    inverse = 1.0 / first_moment
    fade = -0.3 * inverse * (steepness * steepness)
    gain = 0.05 * inverse
    cross = 2.0 * CROSS_FACTOR / (PLUS_FACTOR * MINUS_FACTOR)
    for at, tab, out in ((0, tab_a, mine_out), (PAD, tab_b, other_out)):
        freq = tab[:, 7:8]
        g = stacked_in[at : at + PAD]
        upper = shifted[at : at + PAD]
        lower = shifted[2 * PAD + at : 2 * PAD + at + PAD]
        out[...] = g * (jnp.exp(freq * fade) + (freq * gain) * (g * (upper + lower) - cross * (upper * lower)))


def sources(dev, weights, tabs, sums, pieces, far, start):
    n = pieces[0].shape[1]
    block = BLOCK
    skip = start // block
    spec = lambda rows: pl.BlockSpec((rows, block), lambda i, d: (0, i))
    wide = lambda rows: pl.BlockSpec((rows, block), lambda i, d: (0, i + skip))
    return pl.pallas_call(
        sources_kernel,
        grid_spec=pltpu.PrefetchScalarGridSpec(
            num_scalar_prefetch=1,
            grid=(n // block,),
            in_specs=[pl.BlockSpec((1, 4 * PAD, 3 * PIECES), lambda i, d: (d[0], 0, 0))]
            + [pl.BlockSpec((PAD, TILE), lambda i, d: (0, 0))] * 2
            + [wide(2)] * 3
            + [spec(min(p.shape[0], PAD)) for p in pieces]
            + [wide(FAR)],
            out_specs=[spec(PAD)] * 2,
        ),
        out_shape=[jax.ShapeDtypeStruct((PAD, n), jnp.float32)] * 2,
        compiler_params=SMALL,
        cost_estimate=cost(0),
        name="sources",
    )(dev, weights, *tabs, *sums, *pieces, far)


def expand_kernel(dev_ref, counts_ref, state_ref, *refs):
    count = 2 * len(CHUNKS)
    pieces = refs[:count]
    out_ref, held, room, sems = refs[count:]
    core = dev_ref[0] & 1
    base = 0
    for i, tiles in enumerate(CHUNKS):
        half = tiles // 2
        mine, other = pieces[2 * i], pieces[2 * i + 1]

        def fill(j, _, mine=mine, other=other, base=base, half=half):
            held[base + core * half + j] = mine[:, lanes(j)]
            held[base + (1 - core) * half + j] = other[:, lanes(j)]
            return 0

        lax.fori_loop(0, half, fill, 0, unroll=2)
        base += tiles
    lane = lax.broadcasted_iota(jnp.int32, (PAD, TILE), 1)

    def placed(t, off):
        shift = off & (TILE - 1)
        at = off >> 7
        value = jnp.where(lane >= shift, held[at], held[at + 1])
        value = pltpu.roll(value, (TILE - shift) & (TILE - 1), 1)
        return jnp.where(lane < counts_ref[t], value, 0.0)

    def copy(seg):
        at = pl.ds(pl.multiple_of(seg * (SEG_TILES * TILE), SEG_TILES * TILE), SEG_TILES * TILE)
        return pltpu.make_async_copy(room.at[:, at], out_ref.at[:, at], sems.at[seg])

    def step(g, off):
        values = []
        off = jnp.where(g == state_ref[0], state_ref[1], off)
        for i in range(GROUP):
            t = g * GROUP + i
            values.append(placed(t, off))
            inner = counts_ref[t]
            if i == 0:
                inner = jnp.where(g == 0, 0, inner)
            if i == GROUP - 1:
                inner = jnp.where(g == GROUPS - 1, 0, inner)
            off = off + inner
        for i, value in enumerate(values):
            room[:, lanes(g * GROUP + i)] = value[:ROWS]
        return off

    per = SEG_TILES // GROUP

    def segment(seg, off):
        off = lax.fori_loop(seg * per, seg * per + per, step, off)

        @pl.when((seg > 0) & (seg < SEGMENTS - 1))
        def _():
            copy(seg).start()

        return off

    off = lax.fori_loop(0, SEGMENTS, segment, jnp.int32(0))
    off = jnp.maximum(off, FIRST)
    room[:, lanes(0)] = placed(0, off)[:ROWS]
    copy(0).start()
    off = off + counts_ref[0]
    room[:, lanes(NT - 1)] = placed(NT - 1, off)[:ROWS]
    copy(SEGMENTS - 1).start()
    for seg in range(SEGMENTS):
        copy(seg).wait()


def expand(dev, counts, state, pieces):
    whole = lambda shape: pl.BlockSpec(shape, lambda i, d: (0,) * len(shape))
    return pl.pallas_call(
        expand_kernel,
        grid_spec=pltpu.PrefetchScalarGridSpec(
            num_scalar_prefetch=1,
            grid=(1,),
            in_specs=[SMEM, SMEM] + [whole(p.shape) for p in pieces],
            out_specs=pl.BlockSpec(memory_space=pltpu.HBM),
            scratch_shapes=[
                pltpu.VMEM((SEA_TILES + 4, PAD, TILE), jnp.float32),
                pltpu.VMEM((ROWS, NT * TILE), jnp.float32),
                pltpu.SemaphoreType.DMA((SEGMENTS,)),
            ],
        ),
        out_shape=jax.ShapeDtypeStruct((ROWS, NT * TILE), jnp.float32),
        compiler_params=SMALL,
        cost_estimate=cost(0),
        name="expand",
    )(dev, counts, state, *pieces)


def per_device(spectrum, wind_speed, wind_dir, counts, send_list, neighbors, neighbor_mask):
    dev = lax.axis_index("spec").astype(jnp.int32).reshape(1)
    tab = jnp.asarray(component_params())
    weights = jnp.asarray(interaction_weights())

    def shift(x, hops):
        return lax.ppermute(x, "spec", [(s, (s + hops) % N_SPEC) for s in range(N_SPEC)])

    def cross(x, hops):
        return lax.ppermute(x, "spec", [(s, ((s + hops) % N_SPEC) ^ 1) for s in range(N_SPEC)])

    def swap(x):
        return lax.ppermute(x, "spec", [(s, s ^ 1) for s in range(N_SPEC)])

    to_lower, to_upper, wa, wb, *tabs = edges(dev, spectrum, send_list, wind_speed, wind_dir, tab)
    lower = lax.ppermute(to_upper, "space", [(s, (s + 1) % N_SPACE) for s in range(N_SPACE)])
    upper = lax.ppermute(to_lower, "space", [(s, (s - 1) % N_SPACE) for s in range(N_SPACE)])

    def spread(both):
        up, down = shift(both, 2), shift(both, -2)
        return (up, swap(up[PAD:])), (down, swap(down[PAD:]))

    both1, send, state = advect(
        False, 0, CHUNKS[0], dev, counts, None, spectrum, neighbors, neighbor_mask, wa, wb, tabs[0], [wa]
    )
    up1, down1 = spread(both1)
    own1 = both1, swap(send)
    both2, send = advect(
        True, CHUNKS[0], CHUNKS[1], dev, counts, state, spectrum, neighbors, neighbor_mask, wa, wb, tabs[0],
        [lower, upper, wa],
    )
    up2, down2 = spread(both2)
    own2 = both2, swap(send)
    far = shift(far_pack(dev, own1, own2), -4)
    three, two = moment_windows([(moments(*own1, tabs), up1, down1), (moments(*own2, tabs), up2, down2)], tabs)
    sums = three, shift(three, -6), shift(two, 6)
    relay1 = shift(relay_pack(dev, up1), 2)
    relay2 = shift(relay_pack(dev, up2, [three]), 2)
    results, start = [], 0
    for pieces in ([*own1, *up1, *down1, relay1], [*own2, *up2, *down2, relay2]):
        mine, other = sources(dev, weights, tabs, sums, pieces, far, start)
        start += mine.shape[1]
        results += [mine, swap(other)]
    return expand(dev, counts, state, results)


def solution(mesh):
    in_specs = (
        P("spec", "space"),
        P("space"),
        P("space"),
        P("space"),
        P("space"),
        P(None, "space"),
        P(None, "space"),
    )
    out_specs = P("spec", "space")
    return jax.shard_map(
        per_device, mesh=mesh, in_specs=in_specs, out_specs=out_specs, check_vma=False
    )
```

```python
import math
from functools import partial

import jax
import jax.numpy as jnp
import ml_dtypes
import numpy as np
from jax import lax
from jax.experimental import pallas as pl
from jax.experimental.pallas import tpu as pltpu
from jax.sharding import PartitionSpec as P

ND = 24
NF = 26
TILE = 128
K = 624
NT = 128
ROWS = 39
PAD = 40
CHIPS = 8
CHIP_ROWS = 78
N_SPACE = 16
N_SPEC = 16

LOG_RATIO = math.log(1.1)
FREQ_LOW = 0.05
EPS = 1e-06
PLUS_FACTOR = 1.0 / 1.25**4
MINUS_FACTOR = 1.0 / 0.75**4
CROSS_FACTOR = 1.0 / 0.9375**4

CHUNKS = (40, 40)
FIRST = CHUNKS[0] * TILE
SEA_TILES = sum(CHUNKS)
BLOCK = 1280

RELAY = 24
FAR = 4
PIECES = 6 * PAD + RELAY + 8


def tables():
    k = np.arange(K)
    level = (k // ND).astype(np.float64)
    heading = ((k % ND) + 0.5) * (2.0 * math.pi / ND)
    frequency = FREQ_LOW * np.exp(LOG_RATIO * level)
    courant = 0.6 * np.exp(-LOG_RATIO * level)
    return frequency, heading, courant


FREQ = tables()[0]
MEAN_FREQ = float(FREQ.mean())


def component_params():
    frequency, heading, courant = tables()
    east = courant * np.cos(heading)
    north = courant * np.sin(heading)
    cols = (
        0.08 * frequency * np.cos(heading) / 1.56,
        0.08 * frequency * np.sin(heading) / 1.56,
        np.abs(east),
        np.abs(north),
        1.0 - np.abs(east) - np.abs(north),
        (east > 0).astype(np.float64),
        (north > 0).astype(np.float64),
        frequency,
    )
    out = np.zeros((N_SPEC, PAD, TILE), np.float32)
    for lane, col in enumerate(cols):
        out[:, :ROWS, lane] = col.reshape(N_SPEC, ROWS)
    out[:, :, 8] = np.roll(out[:, :, 7], 2, axis=0)
    out[:, :, 9] = np.roll(out[:, :, 7], -2, axis=0)
    return out


def interaction_table(dir_count, freq_count):
    comp_total = dir_count * freq_count
    matrix = np.zeros((2 * comp_total, comp_total), np.float32)
    shifts = (
        (math.log(1.25) / math.log(1.1), 33.56 * dir_count / 360.0),
        (math.log(0.75) / math.log(1.1), 11.48 * dir_count / 360.0),
    )
    for which_half, (band_shift, turning) in enumerate(shifts):
        for band_level in range(freq_count):
            band_place = band_level + band_shift
            low_band = math.floor(band_place)
            frac_band = band_place - low_band
            for mirror in (1.0, -1.0):
                for heading in range(dir_count):
                    dir_place = heading + mirror * turning
                    low_dir = math.floor(dir_place)
                    frac_dir = dir_place - low_dir
                    row_index = which_half * comp_total + band_level * dir_count + heading
                    for band_step, band_weight in ((0, 1.0 - frac_band), (1, frac_band)):
                        source_band = low_band + band_step
                        if 0 <= source_band < freq_count:
                            for dir_step, dir_weight in ((0, 1.0 - frac_dir), (1, frac_dir)):
                                source_dir = (low_dir + dir_step) % dir_count
                                matrix[row_index, source_band * dir_count + source_dir] += (
                                    0.5 * band_weight * dir_weight
                                )
    return matrix


def piece_columns(dev):
    chip, core = divmod(dev, 2)

    def rows(offset, which):
        first = ((chip + offset) % CHIPS) * CHIP_ROWS + ROWS * which
        return list(range(first, first + ROWS)) + [-1]

    cols = []
    for offset in (0, -1, 1):
        cols += rows(offset, core) + rows(offset, 1 - core)
    below = rows(-2, 1)
    turn = 6 * (chip % 4)
    cols += [below[21 - turn] if turn else -1, -1, -1, -1] + below[20:40]
    above = rows(2, 0)
    turn = 6 * ((chip + 1) % 4)
    cols += (above[9:12] if turn == 6 else above[3:6] if turn == 12 else [-1] * 3) + [-1] * 5
    return cols


def interaction_weights():
    table = interaction_table(ND, NF)
    out = np.zeros((N_SPEC, 4 * PAD, PIECES), np.float32)
    for dev in range(N_SPEC):
        cols = np.array(piece_columns(dev))
        held = cols[cols >= 0]
        assert len(cols) == PIECES and len(set(held.tolist())) == len(held)
        for half, factor in ((0, PLUS_FACTOR), (1, MINUS_FACTOR)):
            for slot, owner in enumerate((dev, dev ^ 1)):
                want = table[half * K + ROWS * owner : half * K + ROWS * owner + ROWS]
                got = np.where(cols >= 0, want[:, np.maximum(cols, 0)], 0.0)
                assert np.array_equal((got != 0).sum(1), (want != 0).sum(1))
                at = half * 2 * PAD + slot * PAD
                out[dev, at : at + ROWS] = got * factor
    high = out.astype(ml_dtypes.bfloat16)
    low = (out - high.astype(np.float32)).astype(ml_dtypes.bfloat16)
    return np.concatenate([high, low, high], axis=2)


VMEM = pl.BlockSpec(memory_space=pltpu.VMEM)
SMEM = pl.BlockSpec(memory_space=pltpu.SMEM)


def cost(us):
    return pl.CostEstimate(flops=0, bytes_accessed=int(us * 3.69e6), transcendentals=0)


PARAMS = pltpu.CompilerParams(vmem_limit_bytes=60 * 1024 * 1024)
SMALL = pltpu.CompilerParams(vmem_limit_bytes=24 * 1024 * 1024)


def lanes(tile):
    return pl.ds(pl.multiple_of(tile * TILE, TILE), TILE)


def gather(x, index):
    return jnp.take_along_axis(x, index, axis=1, mode="promise_in_bounds")


def edges_kernel(dev_ref, first_ref, last_ref, list_ref, speed_ref, dir_ref, tab_ref,
                 low_ref, high_ref, wa_ref, wb_ref, mine_ref, other_ref, sems):
    copies = [
        pltpu.make_async_copy(tab_ref.at[dev_ref[0]], mine_ref, sems.at[0]),
        pltpu.make_async_copy(tab_ref.at[dev_ref[0] ^ 1], other_ref, sems.at[1]),
    ]
    for copy in copies:
        copy.start()
    for src, row, out in ((first_ref, 0, low_ref), (last_ref, 1, high_ref)):
        index = jnp.broadcast_to(list_ref[row : row + 1, :] & (TILE - 1), (PAD, TILE))
        out[...] = gather(src[...], index)
    speed, turn = speed_ref[...], dir_ref[...]
    wa_ref[...] = speed * jnp.cos(turn)
    wb_ref[...] = speed * jnp.sin(turn)
    for copy in copies:
        copy.wait()


def edges(dev, spectrum, send_list, wind_speed, wind_dir, tab):
    whole = lambda rows: pl.BlockSpec((rows, TILE), lambda i, d: (0, 0))
    shape = lambda rows: jax.ShapeDtypeStruct((rows, TILE), jnp.float32)
    return pl.pallas_call(
        edges_kernel,
        grid_spec=pltpu.PrefetchScalarGridSpec(
            num_scalar_prefetch=1,
            grid=(1,),
            in_specs=[
                pl.BlockSpec((PAD, TILE), lambda i, d: (0, 0)),
                pl.BlockSpec((PAD, TILE), lambda i, d: (0, NT - 1)),
                whole(2),
                whole(NT),
                whole(NT),
                pl.BlockSpec(memory_space=pltpu.HBM),
            ],
            out_specs=[whole(PAD)] * 2 + [whole(NT)] * 2 + [whole(PAD)] * 2,
            scratch_shapes=[pltpu.SemaphoreType.DMA((2,))],
        ),
        out_shape=[shape(PAD)] * 2 + [shape(NT)] * 2 + [shape(PAD)] * 2,
        compiler_params=PARAMS,
        cost_estimate=cost(0),
        name="edges",
    )(dev, spectrum, spectrum, send_list.reshape(2, TILE), wind_speed.reshape(NT, TILE), wind_dir.reshape(NT, TILE), tab)


GROUP = 8
GROUPS = NT // GROUP
SEGMENTS = 8
SEG_TILES = NT // SEGMENTS
MARGIN = GROUP + 1


def advect_kernel(last, base, tiles, *refs):
    if last:
        (dev_ref, counts_ref, state_ref, x_hbm, code_hbm, mask_hbm, wa_ref, wb_ref, tab_ref, lower_ref, upper_ref, order_ref,
         both_ref, send_ref, par, dst, x_ref, code_ref, mask_ref, sems) = refs
    else:
        (dev_ref, counts_ref, x_hbm, code_hbm, mask_hbm, wa_ref, wb_ref, tab_ref, order_ref,
         both_ref, send_ref, next_ref, par, dst, x_ref, code_ref, mask_ref, sems) = refs

    def copies(seg):
        at = pl.ds(pl.multiple_of(seg * (SEG_TILES * TILE), SEG_TILES * TILE), SEG_TILES * TILE)
        return (
            pltpu.make_async_copy(x_hbm.at[:, at], x_ref.at[:, at], sems.at[seg, 0]),
            pltpu.make_async_copy(code_hbm.at[:, at], code_ref.at[:, at], sems.at[seg, 1]),
            pltpu.make_async_copy(mask_hbm.at[:, at], mask_ref.at[:, at], sems.at[seg, 2]),
        )

    def start(seg, _):
        for copy in copies(seg):
            copy.start()
        return 0

    def wait(seg, _):
        for copy in copies(seg):
            copy.wait()
        return 0

    if last:
        g0, off0 = state_ref[0], state_ref[1]
        seg0 = jnp.maximum(g0 * GROUP - 1, 0) // SEG_TILES
    else:
        g0, off0, seg0 = jnp.int32(0), jnp.int32(0), jnp.int32(0)
    lax.fori_loop(seg0, SEGMENTS, start, 0)
    if last:
        edge = [
            pltpu.make_async_copy(x_hbm.at[:, pl.ds(0, 2 * TILE)], x_ref.at[:, pl.ds(NT * TILE, 2 * TILE)], sems.at[SEGMENTS, 0]),
            pltpu.make_async_copy(code_hbm.at[:, pl.ds(0, TILE)], code_ref.at[:, pl.ds(NT * TILE, TILE)], sems.at[SEGMENTS, 1]),
            pltpu.make_async_copy(mask_hbm.at[:, pl.ds(0, TILE)], mask_ref.at[:, pl.ds(NT * TILE, TILE)], sems.at[SEGMENTS, 2]),
        ]
        for copy in edge:
            copy.start()

    table = tab_ref[...]
    for i in range(7):
        par[i] = jnp.broadcast_to(table[:ROWS, i : i + 1], (ROWS, TILE))
    lane = lax.broadcasted_iota(jnp.int32, (ROWS, TILE), 1)

    def grown(t, at, before, after):
        own = x_ref[:, at]
        code = code_ref[:, at] & (TILE - 1)
        sea = mask_ref[:, at].astype(jnp.float32)
        to_east = par[5] > 0.5
        to_north = par[6] > 0.5
        near_x = gather(own, jnp.where(to_east, code[0:1], code[1:2]))
        near_x = near_x * jnp.where(to_east, sea[0:1], sea[1:2])
        near_y = gather(jnp.where(to_north, before, after), jnp.where(to_north, code[2:3], code[3:4]))
        near_y = near_y * jnp.where(to_north, sea[2:3], sea[3:4])
        value = own * par[4] + par[2] * near_x + par[3] * near_y
        drive = par[0] * wa_ref[pl.ds(t, 1), :] + par[1] * wb_ref[pl.ds(t, 1), :]
        return value * jnp.exp(jnp.maximum(drive - 0.08, 0.0))

    def store(value, off):
        shift = off & (TILE - 1)
        at = (off >> 7) - base + MARGIN
        dst[at] = jnp.where(lane < shift, dst[at], value)
        dst[at + 1] = value

    def step(g, off):
        values, offs = [], []
        for i in range(GROUP):
            t = g * GROUP + i
            before = x_ref[:, lanes(jnp.maximum(t - 1, 0))]
            after = x_ref[:, lanes(jnp.minimum(t + 1, NT - 1))]
            value = grown(t, lanes(t), before, after)
            values.append(pltpu.roll(value, off & (TILE - 1), 1))
            offs.append(off)
            inner = counts_ref[t]
            if i == 0:
                inner = jnp.where(g == 0, 0, inner)
            if i == GROUP - 1:
                inner = jnp.where(g == GROUPS - 1, 0, inner)
            off = off + inner
        for value, at in zip(values, offs):
            store(value, at)
        return off

    limit = (base + tiles) * TILE

    def body(c):
        g, off, _, ready = c
        need = jnp.minimum((g * GROUP + GROUP) // SEG_TILES, SEGMENTS - 1) + 1
        lax.fori_loop(ready, need, wait, 0)
        return g + 1, step(g, off), off, jnp.maximum(ready, need)

    if last:
        more = lambda c: c[0] < GROUPS
    else:
        total = lax.fori_loop(0, NT, lambda t, n: n + counts_ref[t], jnp.int32(0), unroll=8)
        share, rest = GROUPS * tiles // SEA_TILES, (SEA_TILES - tiles) * TILE
        more = lambda c: (c[0] < GROUPS) & (c[1] < limit) & ((c[0] < share) | (total - c[1] > rest))
    g, off, back, ready = lax.while_loop(
        more,
        body,
        (g0, off0, off0, seg0),
    )
    lax.fori_loop(ready, SEGMENTS, wait, 0)
    if last:
        for copy in edge:
            copy.wait()
        off = jnp.maximum(off, FIRST)
        value = grown(0, pl.ds(NT * TILE, TILE), lower_ref[:ROWS, :], x_ref[:, pl.ds((NT + 1) * TILE, TILE)])
        store(pltpu.roll(value, off & (TILE - 1), 1), off)
        off = off + counts_ref[0]
        value = grown(NT - 1, lanes(NT - 1), x_ref[:, lanes(NT - 2)], upper_ref[:ROWS, :])
        store(pltpu.roll(value, off & (TILE - 1), 1), off)
    else:
        straddles = off > limit
        next_ref[0] = jnp.where(straddles, g - 1, g)
        next_ref[1] = jnp.where(straddles, back, jnp.maximum(off, limit))
    half = tiles // 2
    core = dev_ref[0] & 1

    def emit(j, _):
        other = dst[MARGIN + (1 - core) * half + j]
        both_ref[:ROWS, lanes(j)] = dst[MARGIN + core * half + j]
        both_ref[PAD : PAD + ROWS, lanes(j)] = other
        send_ref[:ROWS, lanes(j)] = other
        return 0

    lax.fori_loop(0, half, emit, 0, unroll=2)
    none = jnp.zeros((PAD - ROWS, send_ref.shape[1]), jnp.float32)
    both_ref[ROWS:PAD, :] = none
    both_ref[PAD + ROWS :, :] = none
    send_ref[ROWS:, :] = none


def advect(last, base, tiles, dev, counts, state, spectrum, codes, mask, wa, wb, tab, extra):
    half = tiles // 2 * TILE
    whole = lambda shape: pl.BlockSpec(shape, lambda i, d: (0,) * len(shape))
    hbm = pl.BlockSpec(memory_space=pltpu.HBM)
    tab_spec = whole((PAD, TILE))
    args = [counts] + ([state] if last else []) + [spectrum, codes, mask, wa, wb, tab] + extra
    specs = [SMEM] + ([SMEM] if last else [])
    specs += [hbm, hbm, hbm, whole((NT, TILE)), whole((NT, TILE)), tab_spec]
    specs += ([whole((PAD, TILE))] * 2 if last else []) + [pl.BlockSpec(memory_space=pl.ANY)]
    outs = [jax.ShapeDtypeStruct((rows, half), jnp.float32) for rows in (2 * PAD, PAD)]
    out_specs = [whole((rows, half)) for rows in (2 * PAD, PAD)]
    if not last:
        outs = outs + [jax.ShapeDtypeStruct((2,), jnp.int32)]
        out_specs = out_specs + [SMEM]
    return pl.pallas_call(
        partial(advect_kernel, last, base, tiles),
        grid_spec=pltpu.PrefetchScalarGridSpec(
            num_scalar_prefetch=1,
            grid=(1,),
            in_specs=specs,
            out_specs=out_specs,
            scratch_shapes=[
                pltpu.VMEM((7, ROWS, TILE), jnp.float32),
                pltpu.VMEM((tiles + 2 * MARGIN + 2, ROWS, TILE), jnp.float32),
                pltpu.VMEM((ROWS, (NT + 2) * TILE), jnp.float32),
                pltpu.VMEM((4, (NT + 2) * TILE), jnp.int32),
                pltpu.VMEM((4, (NT + 2) * TILE), jnp.int32),
                pltpu.SemaphoreType.DMA((SEGMENTS + 1, 3)),
            ],
        ),
        out_shape=outs,
        compiler_params=PARAMS,
        cost_estimate=cost(0),
        name="advect",
    )(dev, *args)


def head(x):
    return pl.BlockSpec((PAD, x.shape[1]), lambda *i: (0, 0))


def moments_kernel(mine_ref, other_ref, tab_a, tab_b, out_ref):
    mine, other = mine_ref[...], other_ref[...]
    fa, fb = tab_a[:, 7:8], tab_b[:, 7:8]
    out_ref[0:1, :] = jnp.sum(mine, axis=0, keepdims=True) + jnp.sum(other, axis=0, keepdims=True)
    out_ref[1:2, :] = jnp.sum(fa * mine, axis=0, keepdims=True) + jnp.sum(fb * other, axis=0, keepdims=True)


def moments(mine, other, tabs):
    n = mine.shape[1]
    return pl.pallas_call(
        moments_kernel,
        grid=(1,),
        in_specs=[head(mine), head(other)] + [pl.BlockSpec((PAD, TILE), lambda i: (0, 0))] * 2,
        out_specs=pl.BlockSpec((2, n), lambda i: (0, 0)),
        out_shape=jax.ShapeDtypeStruct((2, n), jnp.float32),
        compiler_params=SMALL,
        cost_estimate=cost(0),
        name="moments",
    )(mine, other, *tabs)


def windows_kernel(*refs):
    tm, to, three_ref, two_ref = refs[-4:]

    def sums(mine, other, lane):
        fa, fb = tm[:, lane : lane + 1], to[:, lane : lane + 1]
        return (
            jnp.sum(mine, axis=0, keepdims=True) + jnp.sum(other, axis=0, keepdims=True),
            jnp.sum(fa * mine, axis=0, keepdims=True) + jnp.sum(fb * other, axis=0, keepdims=True),
        )

    at = 0
    for j in range(0, len(refs) - 4, 5):
        own, um, uo, dm, do = refs[j : j + 5]
        n = own.shape[1]
        below = sums(um[...], uo[...], 8)
        above = sums(dm[...], do[...], 9)
        for i in range(2):
            two = own[i : i + 1, :] + above[i]
            two_ref[i : i + 1, at : at + n] = two
            three_ref[i : i + 1, at : at + n] = two + below[i]
        at += n


def moment_windows(chunks, tabs):
    args = [x for own, up, down in chunks for x in (own, *up, *down)]
    total = sum(own.shape[1] for own, _, _ in chunks)
    return pl.pallas_call(
        windows_kernel,
        grid=(1,),
        in_specs=[head(x) if x.shape[0] > 2 else pl.BlockSpec(x.shape, lambda i: (0, 0)) for x in args]
        + [pl.BlockSpec((PAD, TILE), lambda i: (0, 0))] * 2,
        out_specs=[pl.BlockSpec((2, total), lambda i: (0, 0))] * 2,
        out_shape=[jax.ShapeDtypeStruct((2, total), jnp.float32)] * 2,
        compiler_params=SMALL,
        cost_estimate=cost(0),
        name="moment_windows",
    )(*args, *tabs)


def far_kernel(dev_ref, *refs):
    out_ref = refs[-1]
    core = dev_ref[0] & 1
    turn = ((dev_ref[0] >> 1) - 1) & 3

    def fill(parts):
        at = 0
        for low in parts:
            n = low.shape[1]
            out_ref[0:3, at : at + n] = jnp.where(turn == 1, low[9:12, :], low[3:6, :])
            out_ref[3:4, at : at + n] = jnp.zeros((1, n), jnp.float32)
            at += n

    @pl.when(core == 0)
    def _():
        fill(refs[0:-1:2])

    @pl.when(core == 1)
    def _():
        fill(refs[1:-1:2])


def far_pack(dev, *pairs):
    total = sum(p[0].shape[1] for p in pairs)
    whole = lambda shape: pl.BlockSpec(shape, lambda i, d: (0, 0))
    return pl.pallas_call(
        far_kernel,
        grid_spec=pltpu.PrefetchScalarGridSpec(
            num_scalar_prefetch=1,
            grid=(1,),
            in_specs=[whole((16, x.shape[1])) for pair in pairs for x in pair],
            out_specs=whole((FAR, total)),
        ),
        out_shape=jax.ShapeDtypeStruct((FAR, total), jnp.float32),
        compiler_params=SMALL,
        cost_estimate=cost(0),
        name="far_pack",
    )(dev, *[x for pair in pairs for x in pair])


def relay_kernel(dev_ref, *refs):
    out_ref = refs[-1]
    core = dev_ref[0] & 1
    turn = ((dev_ref[0] >> 1) + 1) & 3

    def fill(parts):
        at = 0
        for rows in parts:
            n = rows.shape[1]
            row = lambda i: rows[i : i + 1, :]
            out_ref[:, at : at + n] = rows[16:40, :]
            out_ref[0:1, at : at + n] = jnp.where(turn == 1, row(15), jnp.where(turn == 2, row(9), row(3)))
            at += n

    @pl.when(core == 1)
    def _():
        fill(refs[0 : 2 * len(CHUNKS) : 2])

    @pl.when(core == 0)
    def _():
        fill(refs[1 : 2 * len(CHUNKS) : 2])


def relay_pack(dev, ups, after):
    args = [x for up in ups for x in up]
    total = sum(up[0].shape[1] for up in ups)
    return pl.pallas_call(
        relay_kernel,
        grid_spec=pltpu.PrefetchScalarGridSpec(
            num_scalar_prefetch=1,
            grid=(1,),
            in_specs=[head(x) for x in args] + [pl.BlockSpec(memory_space=pl.ANY)] * len(after),
            out_specs=pl.BlockSpec((RELAY, total), lambda i, d: (0, 0)),
        ),
        out_shape=jax.ShapeDtypeStruct((RELAY, total), jnp.float32),
        compiler_params=SMALL,
        cost_estimate=cost(0),
        name="relay_pack",
    )(dev, *args, *after)


def sources_kernel(dev_ref, w_ref, tab_a, tab_b, sum_a, sum_b, sum_c, *refs):
    pieces, (mine_out, other_out) = refs[:-2], refs[-2:]
    far = pieces[-1][...]
    stacked_in = jnp.concatenate([p[...] for p in pieces[:-1]] + [far, jnp.zeros_like(far)], axis=0)
    high = stacked_in.astype(jnp.bfloat16)
    low = (stacked_in - high.astype(jnp.float32)).astype(jnp.bfloat16)
    stacked = jnp.concatenate([high, high, low], axis=0)
    shifted = jnp.dot(w_ref[0], stacked, preferred_element_type=jnp.float32)
    energy_sum = (sum_a[0:1, :] + sum_b[0:1, :] + sum_c[0:1, :]) * (1.0 / K) + EPS
    first_moment = ((sum_a[1:2, :] + sum_b[1:2, :] + sum_c[1:2, :]) * (1.0 / K) + EPS * MEAN_FREQ) / energy_sum
    ratio = first_moment * (1.0 / MEAN_FREQ)
    ratio = ratio * ratio
    steepness = energy_sum * (ratio * ratio)
    inverse = 1.0 / first_moment
    fade = -0.3 * inverse * (steepness * steepness)
    gain = 0.05 * inverse
    cross = 2.0 * CROSS_FACTOR / (PLUS_FACTOR * MINUS_FACTOR)
    for at, tab, out in ((0, tab_a, mine_out), (PAD, tab_b, other_out)):
        freq = tab[:, 7:8]
        g = stacked_in[at : at + PAD]
        upper = shifted[at : at + PAD]
        lower = shifted[2 * PAD + at : 2 * PAD + at + PAD]
        out[...] = g * (jnp.exp(freq * fade) + (freq * gain) * (g * (upper + lower) - cross * (upper * lower)))


def sources(dev, weights, tabs, sums, pieces, relay, far, start):
    n = pieces[0].shape[1]
    block = BLOCK
    skip = start // block
    spec = lambda rows: pl.BlockSpec((rows, block), lambda i, d: (0, i))
    wide = lambda rows: pl.BlockSpec((rows, block), lambda i, d: (0, i + skip))
    return pl.pallas_call(
        sources_kernel,
        grid_spec=pltpu.PrefetchScalarGridSpec(
            num_scalar_prefetch=1,
            grid=(n // block,),
            in_specs=[pl.BlockSpec((1, 4 * PAD, 3 * PIECES), lambda i, d: (d[0], 0, 0))]
            + [pl.BlockSpec((PAD, TILE), lambda i, d: (0, 0))] * 2
            + [wide(2)] * 3
            + [spec(min(p.shape[0], PAD)) for p in pieces]
            + [wide(RELAY), wide(FAR)],
            out_specs=[spec(PAD)] * 2,
        ),
        out_shape=[jax.ShapeDtypeStruct((PAD, n), jnp.float32)] * 2,
        compiler_params=SMALL,
        cost_estimate=cost(0),
        name="sources",
    )(dev, weights, *tabs, *sums, *pieces, relay, far)


def expand_kernel(dev_ref, counts_ref, state_ref, *refs):
    count = 2 * len(CHUNKS)
    pieces = refs[:count]
    out_ref, held, room, sems = refs[count:]
    core = dev_ref[0] & 1
    base = 0
    for i, tiles in enumerate(CHUNKS):
        half = tiles // 2
        mine, other = pieces[2 * i], pieces[2 * i + 1]

        def fill(j, _, mine=mine, other=other, base=base, half=half):
            held[base + core * half + j] = mine[:, lanes(j)]
            held[base + (1 - core) * half + j] = other[:, lanes(j)]
            return 0

        lax.fori_loop(0, half, fill, 0, unroll=2)
        base += tiles
    lane = lax.broadcasted_iota(jnp.int32, (PAD, TILE), 1)

    def placed(t, off):
        shift = off & (TILE - 1)
        at = off >> 7
        value = jnp.where(lane >= shift, held[at], held[at + 1])
        value = pltpu.roll(value, (TILE - shift) & (TILE - 1), 1)
        return jnp.where(lane < counts_ref[t], value, 0.0)

    def copy(seg):
        at = pl.ds(pl.multiple_of(seg * (SEG_TILES * TILE), SEG_TILES * TILE), SEG_TILES * TILE)
        return pltpu.make_async_copy(room.at[:, at], out_ref.at[:, at], sems.at[seg])

    def step(g, off):
        values = []
        off = jnp.where(g == state_ref[0], state_ref[1], off)
        for i in range(GROUP):
            t = g * GROUP + i
            values.append(placed(t, off))
            inner = counts_ref[t]
            if i == 0:
                inner = jnp.where(g == 0, 0, inner)
            if i == GROUP - 1:
                inner = jnp.where(g == GROUPS - 1, 0, inner)
            off = off + inner
        for i, value in enumerate(values):
            room[:, lanes(g * GROUP + i)] = value[:ROWS]
        return off

    per = SEG_TILES // GROUP

    def segment(seg, off):
        off = lax.fori_loop(seg * per, seg * per + per, step, off)

        @pl.when((seg > 0) & (seg < SEGMENTS - 1))
        def _():
            copy(seg).start()

        return off

    off = lax.fori_loop(0, SEGMENTS, segment, jnp.int32(0))
    off = jnp.maximum(off, FIRST)
    room[:, lanes(0)] = placed(0, off)[:ROWS]
    copy(0).start()
    off = off + counts_ref[0]
    room[:, lanes(NT - 1)] = placed(NT - 1, off)[:ROWS]
    copy(SEGMENTS - 1).start()
    for seg in range(SEGMENTS):
        copy(seg).wait()


def expand(dev, counts, state, pieces):
    whole = lambda shape: pl.BlockSpec(shape, lambda i, d: (0,) * len(shape))
    return pl.pallas_call(
        expand_kernel,
        grid_spec=pltpu.PrefetchScalarGridSpec(
            num_scalar_prefetch=1,
            grid=(1,),
            in_specs=[SMEM, SMEM] + [whole(p.shape) for p in pieces],
            out_specs=pl.BlockSpec(memory_space=pltpu.HBM),
            scratch_shapes=[
                pltpu.VMEM((SEA_TILES + 4, PAD, TILE), jnp.float32),
                pltpu.VMEM((ROWS, NT * TILE), jnp.float32),
                pltpu.SemaphoreType.DMA((SEGMENTS,)),
            ],
        ),
        out_shape=jax.ShapeDtypeStruct((ROWS, NT * TILE), jnp.float32),
        compiler_params=SMALL,
        cost_estimate=cost(0),
        name="expand",
    )(dev, counts, state, *pieces)


def per_device(spectrum, wind_speed, wind_dir, counts, send_list, neighbors, neighbor_mask):
    dev = lax.axis_index("spec").astype(jnp.int32).reshape(1)
    tab = jnp.asarray(component_params())
    weights = jnp.asarray(interaction_weights())

    def shift(x, hops):
        return lax.ppermute(x, "spec", [(s, (s + hops) % N_SPEC) for s in range(N_SPEC)])

    def cross(x, hops):
        return lax.ppermute(x, "spec", [(s, ((s + hops) % N_SPEC) ^ 1) for s in range(N_SPEC)])

    def swap(x):
        return lax.ppermute(x, "spec", [(s, s ^ 1) for s in range(N_SPEC)])

    to_lower, to_upper, wa, wb, *tabs = edges(dev, spectrum, send_list, wind_speed, wind_dir, tab)
    lower = lax.ppermute(to_upper, "space", [(s, (s + 1) % N_SPACE) for s in range(N_SPACE)])
    upper = lax.ppermute(to_lower, "space", [(s, (s - 1) % N_SPACE) for s in range(N_SPACE)])

    def spread(both):
        up, down = shift(both, 2), shift(both, -2)
        return (up, swap(up[PAD:])), (down, swap(down[PAD:]))

    both1, send, state = advect(
        False, 0, CHUNKS[0], dev, counts, None, spectrum, neighbors, neighbor_mask, wa, wb, tabs[0], [wa]
    )
    up1, down1 = spread(both1)
    own1 = both1, swap(send)
    both2, send = advect(
        True, CHUNKS[0], CHUNKS[1], dev, counts, state, spectrum, neighbors, neighbor_mask, wa, wb, tabs[0],
        [lower, upper, wa],
    )
    up2, down2 = spread(both2)
    own2 = both2, swap(send)
    far = shift(far_pack(dev, own1, own2), -4)
    three, two = moment_windows([(moments(*own1, tabs), up1, down1), (moments(*own2, tabs), up2, down2)], tabs)
    sums = three, shift(three, -6), shift(two, 6)
    relay = shift(relay_pack(dev, [up1, up2], [three]), 2)
    results, start = [], 0
    for pieces in ([*own1, *up1, *down1], [*own2, *up2, *down2]):
        mine, other = sources(dev, weights, tabs, sums, pieces, relay, far, start)
        start += mine.shape[1]
        results += [mine, swap(other)]
    return expand(dev, counts, state, results)


def solution(mesh):
    in_specs = (
        P("spec", "space"),
        P("space"),
        P("space"),
        P("space"),
        P("space"),
        P(None, "space"),
        P(None, "space"),
    )
    out_specs = P("spec", "space")
    return jax.shard_map(
        per_device, mesh=mesh, in_specs=in_specs, out_specs=out_specs, check_vma=False
    )
```

```python
import math
from functools import partial

import jax
import jax.numpy as jnp
import ml_dtypes
import numpy as np
from jax import lax
from jax.experimental import pallas as pl
from jax.experimental.pallas import tpu as pltpu
from jax.sharding import PartitionSpec as P

ND = 24
NF = 26
TILE = 128
K = 624
NT = 128
ROWS = 39
PAD = 40
CHIPS = 8
CHIP_ROWS = 78
N_SPACE = 16
N_SPEC = 16

LOG_RATIO = math.log(1.1)
FREQ_LOW = 0.05
EPS = 1e-06
PLUS_FACTOR = 1.0 / 1.25**4
MINUS_FACTOR = 1.0 / 0.75**4
CROSS_FACTOR = 1.0 / 0.9375**4

CHUNKS = (40, 40)
FIRST = CHUNKS[0] * TILE
SEA_TILES = sum(CHUNKS)
BLOCK = 1280

RELAY = 24
FAR = 4
PIECES = 6 * PAD + RELAY + 8


def tables():
    k = np.arange(K)
    level = (k // ND).astype(np.float64)
    heading = ((k % ND) + 0.5) * (2.0 * math.pi / ND)
    frequency = FREQ_LOW * np.exp(LOG_RATIO * level)
    courant = 0.6 * np.exp(-LOG_RATIO * level)
    return frequency, heading, courant


FREQ = tables()[0]
MEAN_FREQ = float(FREQ.mean())


def component_params():
    frequency, heading, courant = tables()
    east = courant * np.cos(heading)
    north = courant * np.sin(heading)
    cols = (
        0.08 * frequency * np.cos(heading) / 1.56,
        0.08 * frequency * np.sin(heading) / 1.56,
        np.abs(east),
        np.abs(north),
        1.0 - np.abs(east) - np.abs(north),
        (east > 0).astype(np.float64),
        (north > 0).astype(np.float64),
        frequency,
    )
    out = np.zeros((N_SPEC, PAD, TILE), np.float32)
    for lane, col in enumerate(cols):
        out[:, :ROWS, lane] = col.reshape(N_SPEC, ROWS)
    out[:, :, 8] = np.roll(out[:, :, 7], 2, axis=0)
    out[:, :, 9] = np.roll(out[:, :, 7], -2, axis=0)
    return out


def interaction_table(dir_count, freq_count):
    comp_total = dir_count * freq_count
    matrix = np.zeros((2 * comp_total, comp_total), np.float32)
    shifts = (
        (math.log(1.25) / math.log(1.1), 33.56 * dir_count / 360.0),
        (math.log(0.75) / math.log(1.1), 11.48 * dir_count / 360.0),
    )
    for which_half, (band_shift, turning) in enumerate(shifts):
        for band_level in range(freq_count):
            band_place = band_level + band_shift
            low_band = math.floor(band_place)
            frac_band = band_place - low_band
            for mirror in (1.0, -1.0):
                for heading in range(dir_count):
                    dir_place = heading + mirror * turning
                    low_dir = math.floor(dir_place)
                    frac_dir = dir_place - low_dir
                    row_index = which_half * comp_total + band_level * dir_count + heading
                    for band_step, band_weight in ((0, 1.0 - frac_band), (1, frac_band)):
                        source_band = low_band + band_step
                        if 0 <= source_band < freq_count:
                            for dir_step, dir_weight in ((0, 1.0 - frac_dir), (1, frac_dir)):
                                source_dir = (low_dir + dir_step) % dir_count
                                matrix[row_index, source_band * dir_count + source_dir] += (
                                    0.5 * band_weight * dir_weight
                                )
    return matrix


def piece_columns(dev):
    chip, core = divmod(dev, 2)

    def rows(offset, which):
        first = ((chip + offset) % CHIPS) * CHIP_ROWS + ROWS * which
        return list(range(first, first + ROWS)) + [-1]

    cols = []
    for offset in (0, -1, 1):
        cols += rows(offset, core) + rows(offset, 1 - core)
    below = rows(-2, 1)
    turn = 6 * (chip % 4)
    cols += [below[21 - turn] if turn else -1, -1, -1, -1] + below[20:40]
    above = rows(2, 0)
    turn = 6 * ((chip + 1) % 4)
    cols += (above[9:12] if turn == 6 else above[3:6] if turn == 12 else [-1] * 3) + [-1] * 5
    return cols


def interaction_weights():
    table = interaction_table(ND, NF)
    out = np.zeros((N_SPEC, 4 * PAD, PIECES), np.float32)
    for dev in range(N_SPEC):
        cols = np.array(piece_columns(dev))
        held = cols[cols >= 0]
        assert len(cols) == PIECES and len(set(held.tolist())) == len(held)
        for half, factor in ((0, PLUS_FACTOR), (1, MINUS_FACTOR)):
            for slot, owner in enumerate((dev, dev ^ 1)):
                want = table[half * K + ROWS * owner : half * K + ROWS * owner + ROWS]
                got = np.where(cols >= 0, want[:, np.maximum(cols, 0)], 0.0)
                assert np.array_equal((got != 0).sum(1), (want != 0).sum(1))
                at = half * 2 * PAD + slot * PAD
                out[dev, at : at + ROWS] = got * factor
    high = out.astype(ml_dtypes.bfloat16)
    low = (out - high.astype(np.float32)).astype(ml_dtypes.bfloat16)
    return np.concatenate([high, low, high], axis=2)


VMEM = pl.BlockSpec(memory_space=pltpu.VMEM)
SMEM = pl.BlockSpec(memory_space=pltpu.SMEM)


def cost(us):
    return pl.CostEstimate(flops=0, bytes_accessed=int(us * 3.69e6), transcendentals=0)


PARAMS = pltpu.CompilerParams(vmem_limit_bytes=60 * 1024 * 1024)
SMALL = pltpu.CompilerParams(vmem_limit_bytes=24 * 1024 * 1024)


def lanes(tile):
    return pl.ds(pl.multiple_of(tile * TILE, TILE), TILE)


def gather(x, index):
    return jnp.take_along_axis(x, index, axis=1, mode="promise_in_bounds")


def edges_kernel(dev_ref, first_ref, last_ref, list_ref, speed_ref, dir_ref, tab_ref,
                 low_ref, high_ref, wa_ref, wb_ref, mine_ref, other_ref, sems):
    copies = [
        pltpu.make_async_copy(tab_ref.at[dev_ref[0]], mine_ref, sems.at[0]),
        pltpu.make_async_copy(tab_ref.at[dev_ref[0] ^ 1], other_ref, sems.at[1]),
    ]
    for copy in copies:
        copy.start()
    for src, row, out in ((first_ref, 0, low_ref), (last_ref, 1, high_ref)):
        index = jnp.broadcast_to(list_ref[row : row + 1, :] & (TILE - 1), (PAD, TILE))
        out[...] = gather(src[...], index)
    speed, turn = speed_ref[...], dir_ref[...]
    wa_ref[...] = speed * jnp.cos(turn)
    wb_ref[...] = speed * jnp.sin(turn)
    for copy in copies:
        copy.wait()


def edges(dev, spectrum, send_list, wind_speed, wind_dir, tab):
    whole = lambda rows: pl.BlockSpec((rows, TILE), lambda i, d: (0, 0))
    shape = lambda rows: jax.ShapeDtypeStruct((rows, TILE), jnp.float32)
    return pl.pallas_call(
        edges_kernel,
        grid_spec=pltpu.PrefetchScalarGridSpec(
            num_scalar_prefetch=1,
            grid=(1,),
            in_specs=[
                pl.BlockSpec((PAD, TILE), lambda i, d: (0, 0)),
                pl.BlockSpec((PAD, TILE), lambda i, d: (0, NT - 1)),
                whole(2),
                whole(NT),
                whole(NT),
                pl.BlockSpec(memory_space=pltpu.HBM),
            ],
            out_specs=[whole(PAD)] * 2 + [whole(NT)] * 2 + [whole(PAD)] * 2,
            scratch_shapes=[pltpu.SemaphoreType.DMA((2,))],
        ),
        out_shape=[shape(PAD)] * 2 + [shape(NT)] * 2 + [shape(PAD)] * 2,
        compiler_params=PARAMS,
        cost_estimate=cost(0),
        name="edges",
    )(dev, spectrum, spectrum, send_list.reshape(2, TILE), wind_speed.reshape(NT, TILE), wind_dir.reshape(NT, TILE), tab)


GROUP = 8
GROUPS = NT // GROUP
SEGMENTS = 8
SEG_TILES = NT // SEGMENTS
MARGIN = GROUP + 1


def advect_kernel(last, base, tiles, *refs):
    if last:
        (dev_ref, counts_ref, state_ref, x_hbm, code_hbm, mask_hbm, wa_ref, wb_ref, tab_ref, lower_ref, upper_ref, order_ref,
         both_ref, send_ref, par, dst, x_ref, code_ref, mask_ref, sems) = refs
    else:
        (dev_ref, counts_ref, x_hbm, code_hbm, mask_hbm, wa_ref, wb_ref, tab_ref, order_ref,
         both_ref, send_ref, next_ref, par, dst, x_ref, code_ref, mask_ref, sems) = refs

    def copies(seg):
        at = pl.ds(pl.multiple_of(seg * (SEG_TILES * TILE), SEG_TILES * TILE), SEG_TILES * TILE)
        return (
            pltpu.make_async_copy(x_hbm.at[:, at], x_ref.at[:, at], sems.at[seg, 0]),
            pltpu.make_async_copy(code_hbm.at[:, at], code_ref.at[:, at], sems.at[seg, 1]),
            pltpu.make_async_copy(mask_hbm.at[:, at], mask_ref.at[:, at], sems.at[seg, 2]),
        )

    def start(seg, _):
        for copy in copies(seg):
            copy.start()
        return 0

    def wait(seg, _):
        for copy in copies(seg):
            copy.wait()
        return 0

    if last:
        g0, off0 = state_ref[0], state_ref[1]
        seg0 = jnp.maximum(g0 * GROUP - 1, 0) // SEG_TILES
    else:
        g0, off0, seg0 = jnp.int32(0), jnp.int32(0), jnp.int32(0)
    lax.fori_loop(seg0, SEGMENTS, start, 0)
    if last:
        edge = [
            pltpu.make_async_copy(x_hbm.at[:, pl.ds(0, 2 * TILE)], x_ref.at[:, pl.ds(NT * TILE, 2 * TILE)], sems.at[SEGMENTS, 0]),
            pltpu.make_async_copy(code_hbm.at[:, pl.ds(0, TILE)], code_ref.at[:, pl.ds(NT * TILE, TILE)], sems.at[SEGMENTS, 1]),
            pltpu.make_async_copy(mask_hbm.at[:, pl.ds(0, TILE)], mask_ref.at[:, pl.ds(NT * TILE, TILE)], sems.at[SEGMENTS, 2]),
        ]
        for copy in edge:
            copy.start()

    table = tab_ref[...]
    for i in range(7):
        par[i] = jnp.broadcast_to(table[:ROWS, i : i + 1], (ROWS, TILE))
    lane = lax.broadcasted_iota(jnp.int32, (ROWS, TILE), 1)

    def grown(t, at, before, after):
        own = x_ref[:, at]
        code = code_ref[:, at] & (TILE - 1)
        sea = mask_ref[:, at].astype(jnp.float32)
        to_east = par[5] > 0.5
        to_north = par[6] > 0.5
        near_x = gather(own, jnp.where(to_east, code[0:1], code[1:2]))
        near_x = near_x * jnp.where(to_east, sea[0:1], sea[1:2])
        near_y = gather(jnp.where(to_north, before, after), jnp.where(to_north, code[2:3], code[3:4]))
        near_y = near_y * jnp.where(to_north, sea[2:3], sea[3:4])
        value = own * par[4] + par[2] * near_x + par[3] * near_y
        drive = par[0] * wa_ref[pl.ds(t, 1), :] + par[1] * wb_ref[pl.ds(t, 1), :]
        return value * jnp.exp(jnp.maximum(drive - 0.08, 0.0))

    def store(value, off):
        shift = off & (TILE - 1)
        at = (off >> 7) - base + MARGIN
        dst[at] = jnp.where(lane < shift, dst[at], value)
        dst[at + 1] = value

    def step(g, off):
        values, offs = [], []
        for i in range(GROUP):
            t = g * GROUP + i
            before = x_ref[:, lanes(jnp.maximum(t - 1, 0))]
            after = x_ref[:, lanes(jnp.minimum(t + 1, NT - 1))]
            value = grown(t, lanes(t), before, after)
            values.append(pltpu.roll(value, off & (TILE - 1), 1))
            offs.append(off)
            inner = counts_ref[t]
            if i == 0:
                inner = jnp.where(g == 0, 0, inner)
            if i == GROUP - 1:
                inner = jnp.where(g == GROUPS - 1, 0, inner)
            off = off + inner
        for value, at in zip(values, offs):
            store(value, at)
        return off

    limit = (base + tiles) * TILE

    def body(c):
        g, off, _, ready = c
        need = jnp.minimum((g * GROUP + GROUP) // SEG_TILES, SEGMENTS - 1) + 1
        lax.fori_loop(ready, need, wait, 0)
        return g + 1, step(g, off), off, jnp.maximum(ready, need)

    if last:
        more = lambda c: c[0] < GROUPS
    else:
        total = lax.fori_loop(0, NT, lambda t, n: n + counts_ref[t], jnp.int32(0), unroll=8)
        share, rest = GROUPS * tiles // SEA_TILES, (SEA_TILES - tiles) * TILE
        more = lambda c: (c[0] < GROUPS) & (c[1] < limit) & ((c[0] < share) | (total - c[1] > rest))
    g, off, back, ready = lax.while_loop(
        more,
        body,
        (g0, off0, off0, seg0),
    )
    lax.fori_loop(ready, SEGMENTS, wait, 0)
    if last:
        for copy in edge:
            copy.wait()
        off = jnp.maximum(off, FIRST)
        value = grown(0, pl.ds(NT * TILE, TILE), lower_ref[:ROWS, :], x_ref[:, pl.ds((NT + 1) * TILE, TILE)])
        store(pltpu.roll(value, off & (TILE - 1), 1), off)
        off = off + counts_ref[0]
        value = grown(NT - 1, lanes(NT - 1), x_ref[:, lanes(NT - 2)], upper_ref[:ROWS, :])
        store(pltpu.roll(value, off & (TILE - 1), 1), off)
    else:
        straddles = off > limit
        next_ref[0] = jnp.where(straddles, g - 1, g)
        next_ref[1] = jnp.where(straddles, back, jnp.maximum(off, limit))
    half = tiles // 2
    core = dev_ref[0] & 1

    def emit(j, _):
        other = dst[MARGIN + (1 - core) * half + j]
        both_ref[:ROWS, lanes(j)] = dst[MARGIN + core * half + j]
        both_ref[PAD : PAD + ROWS, lanes(j)] = other
        send_ref[:ROWS, lanes(j)] = other
        return 0

    lax.fori_loop(0, half, emit, 0, unroll=10)
    none = jnp.zeros((PAD - ROWS, send_ref.shape[1]), jnp.float32)
    both_ref[ROWS:PAD, :] = none
    both_ref[PAD + ROWS :, :] = none
    send_ref[ROWS:, :] = none


def advect(last, base, tiles, dev, counts, state, spectrum, codes, mask, wa, wb, tab, extra):
    half = tiles // 2 * TILE
    whole = lambda shape: pl.BlockSpec(shape, lambda i, d: (0,) * len(shape))
    hbm = pl.BlockSpec(memory_space=pltpu.HBM)
    tab_spec = whole((PAD, TILE))
    args = [counts] + ([state] if last else []) + [spectrum, codes, mask, wa, wb, tab] + extra
    specs = [SMEM] + ([SMEM] if last else [])
    specs += [hbm, hbm, hbm, whole((NT, TILE)), whole((NT, TILE)), tab_spec]
    specs += ([whole((PAD, TILE))] * 2 if last else []) + [pl.BlockSpec(memory_space=pl.ANY)]
    outs = [jax.ShapeDtypeStruct((rows, half), jnp.float32) for rows in (2 * PAD, PAD)]
    out_specs = [whole((rows, half)) for rows in (2 * PAD, PAD)]
    if not last:
        outs = outs + [jax.ShapeDtypeStruct((2,), jnp.int32)]
        out_specs = out_specs + [SMEM]
    return pl.pallas_call(
        partial(advect_kernel, last, base, tiles),
        grid_spec=pltpu.PrefetchScalarGridSpec(
            num_scalar_prefetch=1,
            grid=(1,),
            in_specs=specs,
            out_specs=out_specs,
            scratch_shapes=[
                pltpu.VMEM((7, ROWS, TILE), jnp.float32),
                pltpu.VMEM((tiles + 2 * MARGIN + 2, ROWS, TILE), jnp.float32),
                pltpu.VMEM((ROWS, (NT + 2) * TILE), jnp.float32),
                pltpu.VMEM((4, (NT + 2) * TILE), jnp.int32),
                pltpu.VMEM((4, (NT + 2) * TILE), jnp.int32),
                pltpu.SemaphoreType.DMA((SEGMENTS + 1, 3)),
            ],
        ),
        out_shape=outs,
        compiler_params=PARAMS,
        cost_estimate=cost(0),
        name="advect",
    )(dev, *args)


def head(x):
    return pl.BlockSpec((PAD, x.shape[1]), lambda *i: (0, 0))


def moments_kernel(mine_ref, other_ref, tab_a, tab_b, out_ref):
    mine, other = mine_ref[...], other_ref[...]
    fa, fb = tab_a[:, 7:8], tab_b[:, 7:8]
    out_ref[0:1, :] = jnp.sum(mine, axis=0, keepdims=True) + jnp.sum(other, axis=0, keepdims=True)
    out_ref[1:2, :] = jnp.sum(fa * mine, axis=0, keepdims=True) + jnp.sum(fb * other, axis=0, keepdims=True)


def moments(mine, other, tabs):
    n = mine.shape[1]
    return pl.pallas_call(
        moments_kernel,
        grid=(1,),
        in_specs=[head(mine), head(other)] + [pl.BlockSpec((PAD, TILE), lambda i: (0, 0))] * 2,
        out_specs=pl.BlockSpec((2, n), lambda i: (0, 0)),
        out_shape=jax.ShapeDtypeStruct((2, n), jnp.float32),
        compiler_params=SMALL,
        cost_estimate=cost(0),
        name="moments",
    )(mine, other, *tabs)


def windows_kernel(*refs):
    tm, to, three_ref, two_ref = refs[-4:]

    def sums(mine, other, lane):
        fa, fb = tm[:, lane : lane + 1], to[:, lane : lane + 1]
        return (
            jnp.sum(mine, axis=0, keepdims=True) + jnp.sum(other, axis=0, keepdims=True),
            jnp.sum(fa * mine, axis=0, keepdims=True) + jnp.sum(fb * other, axis=0, keepdims=True),
        )

    at = 0
    for j in range(0, len(refs) - 4, 5):
        own, um, uo, dm, do = refs[j : j + 5]
        n = own.shape[1]
        below = sums(um[...], uo[...], 8)
        above = sums(dm[...], do[...], 9)
        for i in range(2):
            two = own[i : i + 1, :] + above[i]
            two_ref[i : i + 1, at : at + n] = two
            three_ref[i : i + 1, at : at + n] = two + below[i]
        at += n


def moment_windows(chunks, tabs):
    args = [x for own, up, down in chunks for x in (own, *up, *down)]
    total = sum(own.shape[1] for own, _, _ in chunks)
    return pl.pallas_call(
        windows_kernel,
        grid=(1,),
        in_specs=[head(x) if x.shape[0] > 2 else pl.BlockSpec(x.shape, lambda i: (0, 0)) for x in args]
        + [pl.BlockSpec((PAD, TILE), lambda i: (0, 0))] * 2,
        out_specs=[pl.BlockSpec((2, total), lambda i: (0, 0))] * 2,
        out_shape=[jax.ShapeDtypeStruct((2, total), jnp.float32)] * 2,
        compiler_params=SMALL,
        cost_estimate=cost(0),
        name="moment_windows",
    )(*args, *tabs)


def far_kernel(dev_ref, *refs):
    out_ref = refs[-1]
    core = dev_ref[0] & 1
    turn = ((dev_ref[0] >> 1) - 1) & 3

    def fill(parts):
        at = 0
        for low in parts:
            n = low.shape[1]
            out_ref[0:3, at : at + n] = jnp.where(turn == 1, low[9:12, :], low[3:6, :])
            out_ref[3:4, at : at + n] = jnp.zeros((1, n), jnp.float32)
            at += n

    @pl.when(core == 0)
    def _():
        fill(refs[0:-1:2])

    @pl.when(core == 1)
    def _():
        fill(refs[1:-1:2])


def far_pack(dev, *pairs):
    total = sum(p[0].shape[1] for p in pairs)
    whole = lambda shape: pl.BlockSpec(shape, lambda i, d: (0, 0))
    return pl.pallas_call(
        far_kernel,
        grid_spec=pltpu.PrefetchScalarGridSpec(
            num_scalar_prefetch=1,
            grid=(1,),
            in_specs=[whole((16, x.shape[1])) for pair in pairs for x in pair],
            out_specs=whole((FAR, total)),
        ),
        out_shape=jax.ShapeDtypeStruct((FAR, total), jnp.float32),
        compiler_params=SMALL,
        cost_estimate=cost(0),
        name="far_pack",
    )(dev, *[x for pair in pairs for x in pair])


def relay_kernel(dev_ref, mine_ref, other_ref, *refs):
    out_ref = refs[-1]
    core = dev_ref[0] & 1
    turn = ((dev_ref[0] >> 1) + 1) & 3

    def fill(rows):
        row = lambda i: rows[i : i + 1, :]
        out_ref[...] = rows[16:40, :]
        out_ref[0:1, :] = jnp.where(turn == 1, row(15), jnp.where(turn == 2, row(9), row(3)))

    @pl.when(core == 1)
    def _():
        fill(mine_ref)

    @pl.when(core == 0)
    def _():
        fill(other_ref)


def relay_pack(dev, up, after=()):
    n = up[0].shape[1]
    return pl.pallas_call(
        relay_kernel,
        grid_spec=pltpu.PrefetchScalarGridSpec(
            num_scalar_prefetch=1,
            grid=(1,),
            in_specs=[head(x) for x in up]
            + [pl.BlockSpec(memory_space=pl.ANY)] * len(after),
            out_specs=pl.BlockSpec((RELAY, n), lambda i, d: (0, 0)),
        ),
        out_shape=jax.ShapeDtypeStruct((RELAY, n), jnp.float32),
        compiler_params=SMALL,
        cost_estimate=cost(0),
        name="relay_pack",
    )(dev, *up, *after)


def sources_kernel(dev_ref, w_ref, tab_a, tab_b, sum_a, sum_b, sum_c, *refs):
    pieces, (mine_out, other_out) = refs[:-2], refs[-2:]
    far = pieces[-1][...]
    stacked_in = jnp.concatenate([p[...] for p in pieces[:-1]] + [far, jnp.zeros_like(far)], axis=0)
    high = stacked_in.astype(jnp.bfloat16)
    low = (stacked_in - high.astype(jnp.float32)).astype(jnp.bfloat16)
    stacked = jnp.concatenate([high, high, low], axis=0)
    shifted = jnp.dot(w_ref[0], stacked, preferred_element_type=jnp.float32)
    energy_sum = (sum_a[0:1, :] + sum_b[0:1, :] + sum_c[0:1, :]) * (1.0 / K) + EPS
    first_moment = ((sum_a[1:2, :] + sum_b[1:2, :] + sum_c[1:2, :]) * (1.0 / K) + EPS * MEAN_FREQ) / energy_sum
    ratio = first_moment * (1.0 / MEAN_FREQ)
    ratio = ratio * ratio
    steepness = energy_sum * (ratio * ratio)
    inverse = 1.0 / first_moment
    fade = -0.3 * inverse * (steepness * steepness)
    gain = 0.05 * inverse
    cross = 2.0 * CROSS_FACTOR / (PLUS_FACTOR * MINUS_FACTOR)
    for at, tab, out in ((0, tab_a, mine_out), (PAD, tab_b, other_out)):
        freq = tab[:, 7:8]
        g = stacked_in[at : at + PAD]
        upper = shifted[at : at + PAD]
        lower = shifted[2 * PAD + at : 2 * PAD + at + PAD]
        out[...] = g * (jnp.exp(freq * fade) + (freq * gain) * (g * (upper + lower) - cross * (upper * lower)))


def sources(dev, weights, tabs, sums, pieces, far, start):
    n = pieces[0].shape[1]
    block = BLOCK
    skip = start // block
    spec = lambda rows: pl.BlockSpec((rows, block), lambda i, d: (0, i))
    wide = lambda rows: pl.BlockSpec((rows, block), lambda i, d: (0, i + skip))
    return pl.pallas_call(
        sources_kernel,
        grid_spec=pltpu.PrefetchScalarGridSpec(
            num_scalar_prefetch=1,
            grid=(n // block,),
            in_specs=[pl.BlockSpec((1, 4 * PAD, 3 * PIECES), lambda i, d: (d[0], 0, 0))]
            + [pl.BlockSpec((PAD, TILE), lambda i, d: (0, 0))] * 2
            + [wide(2)] * 3
            + [spec(min(p.shape[0], PAD)) for p in pieces]
            + [wide(FAR)],
            out_specs=[spec(PAD)] * 2,
        ),
        out_shape=[jax.ShapeDtypeStruct((PAD, n), jnp.float32)] * 2,
        compiler_params=SMALL,
        cost_estimate=cost(0),
        name="sources",
    )(dev, weights, *tabs, *sums, *pieces, far)


def expand_kernel(dev_ref, counts_ref, state_ref, *refs):
    count = 2 * len(CHUNKS)
    pieces = refs[:count]
    out_ref, held, room, sems = refs[count:]
    core = dev_ref[0] & 1
    base = 0
    for i, tiles in enumerate(CHUNKS):
        half = tiles // 2
        mine, other = pieces[2 * i], pieces[2 * i + 1]

        def fill(j, _, mine=mine, other=other, base=base, half=half):
            held[base + core * half + j] = mine[:, lanes(j)]
            held[base + (1 - core) * half + j] = other[:, lanes(j)]
            return 0

        lax.fori_loop(0, half, fill, 0, unroll=10)
        base += tiles
    lane = lax.broadcasted_iota(jnp.int32, (PAD, TILE), 1)

    def placed(t, off):
        shift = off & (TILE - 1)
        at = off >> 7
        value = jnp.where(lane >= shift, held[at], held[at + 1])
        value = pltpu.roll(value, (TILE - shift) & (TILE - 1), 1)
        return jnp.where(lane < counts_ref[t], value, 0.0)

    def copy(seg):
        at = pl.ds(pl.multiple_of(seg * (SEG_TILES * TILE), SEG_TILES * TILE), SEG_TILES * TILE)
        return pltpu.make_async_copy(room.at[:, at], out_ref.at[:, at], sems.at[seg])

    def step(g, off):
        values = []
        off = jnp.where(g == state_ref[0], state_ref[1], off)
        for i in range(GROUP):
            t = g * GROUP + i
            values.append(placed(t, off))
            inner = counts_ref[t]
            if i == 0:
                inner = jnp.where(g == 0, 0, inner)
            if i == GROUP - 1:
                inner = jnp.where(g == GROUPS - 1, 0, inner)
            off = off + inner
        for i, value in enumerate(values):
            room[:, lanes(g * GROUP + i)] = value[:ROWS]
        return off

    per = SEG_TILES // GROUP

    def segment(seg, off):
        off = lax.fori_loop(seg * per, seg * per + per, step, off)

        @pl.when((seg > 0) & (seg < SEGMENTS - 1))
        def _():
            copy(seg).start()

        return off

    off = lax.fori_loop(0, SEGMENTS, segment, jnp.int32(0))
    off = jnp.maximum(off, FIRST)
    room[:, lanes(0)] = placed(0, off)[:ROWS]
    copy(0).start()
    off = off + counts_ref[0]
    room[:, lanes(NT - 1)] = placed(NT - 1, off)[:ROWS]
    copy(SEGMENTS - 1).start()
    for seg in range(SEGMENTS):
        copy(seg).wait()


def expand(dev, counts, state, pieces):
    whole = lambda shape: pl.BlockSpec(shape, lambda i, d: (0,) * len(shape))
    return pl.pallas_call(
        expand_kernel,
        grid_spec=pltpu.PrefetchScalarGridSpec(
            num_scalar_prefetch=1,
            grid=(1,),
            in_specs=[SMEM, SMEM] + [whole(p.shape) for p in pieces],
            out_specs=pl.BlockSpec(memory_space=pltpu.HBM),
            scratch_shapes=[
                pltpu.VMEM((SEA_TILES + 4, PAD, TILE), jnp.float32),
                pltpu.VMEM((ROWS, NT * TILE), jnp.float32),
                pltpu.SemaphoreType.DMA((SEGMENTS,)),
            ],
        ),
        out_shape=jax.ShapeDtypeStruct((ROWS, NT * TILE), jnp.float32),
        compiler_params=SMALL,
        cost_estimate=cost(0),
        name="expand",
    )(dev, counts, state, *pieces)


def per_device(spectrum, wind_speed, wind_dir, counts, send_list, neighbors, neighbor_mask):
    dev = lax.axis_index("spec").astype(jnp.int32).reshape(1)
    tab = jnp.asarray(component_params())
    weights = jnp.asarray(interaction_weights())

    def shift(x, hops):
        return lax.ppermute(x, "spec", [(s, (s + hops) % N_SPEC) for s in range(N_SPEC)])

    def cross(x, hops):
        return lax.ppermute(x, "spec", [(s, ((s + hops) % N_SPEC) ^ 1) for s in range(N_SPEC)])

    def swap(x):
        return lax.ppermute(x, "spec", [(s, s ^ 1) for s in range(N_SPEC)])

    to_lower, to_upper, wa, wb, *tabs = edges(dev, spectrum, send_list, wind_speed, wind_dir, tab)
    lower = lax.ppermute(to_upper, "space", [(s, (s + 1) % N_SPACE) for s in range(N_SPACE)])
    upper = lax.ppermute(to_lower, "space", [(s, (s - 1) % N_SPACE) for s in range(N_SPACE)])

    def spread(both):
        up, down = shift(both, 2), shift(both, -2)
        return (up, swap(up[PAD:])), (down, swap(down[PAD:]))

    both1, send, state = advect(
        False, 0, CHUNKS[0], dev, counts, None, spectrum, neighbors, neighbor_mask, wa, wb, tabs[0], [wa]
    )
    up1, down1 = spread(both1)
    own1 = both1, swap(send)
    both2, send = advect(
        True, CHUNKS[0], CHUNKS[1], dev, counts, state, spectrum, neighbors, neighbor_mask, wa, wb, tabs[0],
        [lower, upper, wa],
    )
    up2, down2 = spread(both2)
    own2 = both2, swap(send)
    far = shift(far_pack(dev, own1, own2), -4)
    three, two = moment_windows([(moments(*own1, tabs), up1, down1), (moments(*own2, tabs), up2, down2)], tabs)
    sums = three, shift(three, -6), shift(two, 6)
    relay1 = shift(relay_pack(dev, up1), 2)
    relay2 = shift(relay_pack(dev, up2, [three]), 2)
    results, start = [], 0
    for pieces in ([*own1, *up1, *down1, relay1], [*own2, *up2, *down2, relay2]):
        mine, other = sources(dev, weights, tabs, sums, pieces, far, start)
        start += mine.shape[1]
        results += [mine, swap(other)]
    return expand(dev, counts, state, results)


def solution(mesh):
    in_specs = (
        P("spec", "space"),
        P("space"),
        P("space"),
        P("space"),
        P("space"),
        P(None, "space"),
        P(None, "space"),
    )
    out_specs = P("spec", "space")
    return jax.shard_map(
        per_device, mesh=mesh, in_specs=in_specs, out_specs=out_specs, check_vma=False
    )
```
